128 devices in a mesh: node: 32 (over z, y, x_hi), local: 4 (over x_lo, core).
Axes of the slice: x: 4 (x_hi: 2, x_lo: 2; x = x_hi * 2 + x_lo), y: 4, z: 4, core: 2. Of those that a mesh axis runs over, the one named last changes fastest.
Arguments:
- tokens: bfloat16 [8192, 7168], P('node', 'local'), may hold values from -6 to 6
- expert_ids: int32 [8192, 8], P('node'), may hold values from 0 to 255, as said below
- keep_flags: int32 [8192, 8], P('node'), may hold values 0 or 1
- affinity: float32 [8192, 8], P('node'), may hold values from 0.05 to 1
- w_gate: bfloat16 [32, 7168, 1024], P('node', 'local'), may hold values from -0.0625 to 0.0625
- w_up: bfloat16 [32, 7168, 1024], P('node', 'local'), may hold values from -0.0625 to 0.0625
- w_down: bfloat16 [32, 1024, 7168], P('node', None, 'local'), may hold values from -0.1875 to 0.1875
- cotangent: bfloat16 [8192, 7168], P('node', 'local'), may hold values from -6 to 6
Outputs:
- mixed: bfloat16 [8192, 7168], P('node', 'local')
- token_grad: bfloat16 [8192, 7168], P('node', 'local')
- affinity_grad: float32 [8192, 8], P('node')
The draws below stay inside these ranges and needn't reach their ends.
Inputs may be any that keep to these rules, and one draw needn't show every extreme that they name: `expert_ids`: each row names 8 different experts, all within at most 4 of the 8 groups of consecutive experts.
All inputs are finite; a program needn't handle non-finite values. No bound on the sum of `keep_flags` on one device may be relied on, other than what follows from the above.
Results may differ from the reference program's by a relative error of at most 0.04.
Values may be sent and summed in bfloat16 or wider, within the bound.
No kernel may reach another device: no remote copies, remote signals or barrier semaphores. Data moves between devices by JAX's collectives and lax.ppermute only.
A program may use at most 128 MiB of HBM per device.

```python
import math
import jax
import jax.numpy as jnp
from jax import lax

D = 7168
FF = 1024
EXPERTS = 256
GROUPS = 8
TOP_GROUPS = 4
TOP = 8
TOK_NODE = 256
CAP = 10
FLIGHT = 32
STRIDE = 8
TOKENS = 8192
N_LOCAL = 4


def draw_expert_ids(key, part):
    key = jax.random.fold_in(key, 11)
    first, second, third = jax.random.split(key, 3)
    per_group = EXPERTS // GROUPS
    favored = STRIDE * jax.random.randint(first, (), 0, EXPERTS // STRIDE, dtype=jnp.int32)
    favored_group = favored // per_group
    forced = jnp.arange(TOKENS, dtype=jnp.int32) % 16 < 4
    group_index = jnp.arange(GROUPS, dtype=jnp.int32)
    group_score = jax.random.randint(second, (TOKENS, GROUPS), 0, 1 << 20, dtype=jnp.int32) * GROUPS + group_index
    group_score = jnp.where(forced[:, None] & (group_index == favored_group)[None, :], 1 << 27, group_score)
    unused, chosen = lax.top_k(group_score, TOP_GROUPS)
    allowed = jnp.any(chosen[:, :, None] == group_index[None, None, :], axis=1)
    expert_index = jnp.arange(EXPERTS, dtype=jnp.int32)
    expert_score = jax.random.randint(third, (TOKENS, EXPERTS), 0, 1 << 16, dtype=jnp.int32) * EXPERTS + expert_index
    expert_allowed = jnp.take(allowed, expert_index // per_group, axis=1)
    expert_score = jnp.where(expert_allowed, expert_score, -1 - expert_index)
    expert_score = jnp.where(forced[:, None] & (expert_index == favored)[None, :], 1 << 27, expert_score)
    unused_two, picked = lax.top_k(expert_score, TOP)
    return picked.astype(jnp.int32)


def with_ends(values, key, low, largest):
    extent = values.shape
    place = [jax.random.randint(jax.random.fold_in(key, axis), (), 0, extent[axis]) for axis in range(len(extent))]
    values = values.at[tuple(place)].set(low)
    longest = extent.index(max(extent))
    place[longest] = (place[longest] + 1) % extent[longest]
    return values.at[tuple(place)].set(largest)


def steps_of(stream_key, extent, cuts, least, high):
    factor_of, own = 1.0, jax.random.fold_in(stream_key, 6)
    for axis_at, blocks in cuts:
        draws = jnp.exp(jax.random.uniform(jax.random.fold_in(own, axis_at), (blocks,), jnp.float32, least / len(cuts), high / len(cuts)))
        factor_of = factor_of * jnp.repeat(draws, extent[axis_at] // blocks).reshape([-1 if axis == axis_at else 1 for axis in range(len(extent))])
    return factor_of


def scatter_about(rng, shape, scale, most, cuts=(), held_as=jnp.bfloat16):
    gain = steps_of(rng, shape, cuts, -0.22, 0.18) if cuts else 1.0
    values = jax.random.normal(rng, shape, jnp.float32) * scale * gain
    return jnp.minimum(jnp.maximum(values, -most), most).astype(held_as)


def setup_inputs(seed: int = 0) -> dict:
    seeds = jax.random.split(jax.random.key(seed), 9)
    tokens = scatter_about(seeds[0], (TOKENS, D), 1.0, 6.0, ((0, 32), (1, 4)))
    expert_ids = draw_expert_ids(jax.random.fold_in(seeds[8], 71), 0)
    keep_flags = with_ends((jax.random.randint(seeds[2], (TOKENS, TOP), 0, 8) < 5).astype(jnp.int32), jax.random.fold_in(seeds[2], 1), 0, 1)
    affinity = jnp.clip(jnp.exp(math.log(1.0) - 2.9957323 * jax.random.uniform(seeds[3], (TOKENS, TOP), jnp.float32) ** steps_of(seeds[3], (TOKENS, TOP), ((0, 32),), -0.2, 0.2)), 0.05, 1.0)
    w_gate = scatter_about(seeds[4], (FLIGHT, D, FF), D ** -0.5, 0.0625, ((0, 32), (1, 4)))
    w_up = scatter_about(seeds[5], (FLIGHT, D, FF), D ** -0.5, 0.0625, ((0, 32), (1, 4)))
    w_down = scatter_about(seeds[6], (FLIGHT, FF, D), FF ** -0.5, 0.1875, ((0, 32), (2, 4)))
    cotangent = scatter_about(seeds[7], (TOKENS, D), 1.0, 6.0, ((0, 32), (1, 4)))
    return {"tokens": tokens, "expert_ids": expert_ids, "keep_flags": keep_flags, "affinity": affinity, "w_gate": w_gate, "w_up": w_up, "w_down": w_down, "cotangent": cotangent}


route_scale = 2.5


def route_table(expert_ids, keep_flags):
    live = (keep_flags == 1) & (expert_ids % STRIDE == 0)
    target = (expert_ids // STRIDE).astype(jnp.int32)
    onehot = ((target[..., None] == jnp.arange(FLIGHT, dtype=jnp.int32)) & live[..., None]).astype(jnp.int32)
    blocked = onehot.reshape(FLIGHT, TOK_NODE * TOP, FLIGHT)
    earlier = (jnp.cumsum(blocked, axis=1) - blocked).astype(jnp.int32)
    position = jnp.sum(earlier * blocked, axis=2).astype(jnp.int32).reshape(TOKENS, TOP)
    routed = live & (position < CAP)
    block_of = (jnp.arange(TOKENS, dtype=jnp.int32) // TOK_NODE)[:, None]
    destination = jnp.where(routed, target * (FLIGHT * CAP) + block_of * CAP + position, FLIGHT * FLIGHT * CAP)
    return destination.astype(jnp.int32)


def reference(tokens, expert_ids, keep_flags, affinity, w_gate, w_up, w_down, cotangent):
    destination = route_table(expert_ids, keep_flags)
    total_slots = FLIGHT * FLIGHT * CAP
    route_rows = jnp.full((total_slots,), TOKENS * TOP, jnp.int32)
    route_rows = route_rows.at[destination.reshape(-1)].set(jnp.arange(TOKENS * TOP, dtype=jnp.int32), mode="drop")
    token_rows = (route_rows // TOP).astype(jnp.int32)
    total = jnp.sum(affinity, axis=1, keepdims=True)
    weight = route_scale * affinity / total
    width_local = D // N_LOCAL
    tokens_pad = jnp.concatenate([tokens, jnp.zeros((1, D), tokens.dtype)], axis=0)
    cot_pad = jnp.concatenate([cotangent, jnp.zeros((1, D), cotangent.dtype)], axis=0)
    weight_pad = jnp.concatenate([weight.reshape(-1), jnp.zeros((1,), weight.dtype)])
    rows_each = FLIGHT * CAP

    def expert_pass(operands):
        token_row, route_row, gate_e, up_e, down_e = operands
        rows_in = jnp.take(tokens_pad, token_row, axis=0)
        grads_in = (jnp.take(weight_pad, route_row)[:, None] * jnp.take(cot_pad, token_row, axis=0).astype(jnp.float32)).astype(jnp.bfloat16)
        paired = jnp.concatenate([gate_e, up_e], axis=1)
        split_rows = rows_in.astype(jnp.float32).reshape(rows_each, N_LOCAL, width_local).transpose(1, 0, 2)
        split_pair = paired.astype(jnp.float32).reshape(N_LOCAL, width_local, 2 * FF)
        partial_pre = jnp.einsum("lrd,ldf->lrf", split_rows, split_pair, precision=lax.Precision.HIGHEST)
        rounded = lax.optimization_barrier(partial_pre.astype(jnp.bfloat16))
        pre = jnp.sum(rounded.astype(jnp.float32), axis=0)
        gate_pre = pre[:, :FF]
        up_pre = pre[:, FF:]
        sigma = jax.nn.sigmoid(gate_pre)
        hidden = (gate_pre * sigma * up_pre).astype(jnp.bfloat16)
        rows_out = jnp.dot(hidden, down_e, preferred_element_type=jnp.float32).astype(jnp.bfloat16)
        split_grads = grads_in.astype(jnp.float32).reshape(rows_each, N_LOCAL, width_local).transpose(1, 0, 2)
        split_down = down_e.astype(jnp.float32).reshape(FF, N_LOCAL, width_local).transpose(1, 0, 2)
        partial_grad = jnp.einsum("lrd,lfd->lrf", split_grads, split_down, precision=lax.Precision.HIGHEST)
        rounded_grad = lax.optimization_barrier(partial_grad.astype(jnp.bfloat16))
        hidden_grad = jnp.sum(rounded_grad.astype(jnp.float32), axis=0)
        gate_grad = (hidden_grad * up_pre * sigma * (1.0 + gate_pre * (1.0 - sigma))).astype(jnp.bfloat16)
        up_grad = (hidden_grad * gate_pre * sigma).astype(jnp.bfloat16)
        pair_grad = jnp.concatenate([gate_grad, up_grad], axis=1)
        rows_back = lax.dot_general(pair_grad, paired, (((1,), (1,)), ((), ())), preferred_element_type=jnp.float32).astype(jnp.bfloat16)
        return rows_out, rows_back

    outs_all, backs_all = lax.map(expert_pass, (token_rows.reshape(FLIGHT, rows_each), route_rows.reshape(FLIGHT, rows_each), w_gate, w_up, w_down))
    out_flat = jnp.concatenate([outs_all.reshape(total_slots, D), jnp.zeros((1, D), jnp.bfloat16)], axis=0)
    back_flat = jnp.concatenate([backs_all.reshape(total_slots, D), jnp.zeros((1, D), jnp.bfloat16)], axis=0)
    cot_wide = cotangent.astype(jnp.float32)
    mixed = jnp.zeros((TOKENS, D), jnp.float32)
    grads = jnp.zeros((TOKENS, D), jnp.float32)
    inner_list = []
    for column in range(TOP):
        picked = jnp.take(out_flat, destination[:, column], axis=0).astype(jnp.float32)
        mixed = mixed + weight[:, column:column + 1] * picked
        grads = grads + jnp.take(back_flat, destination[:, column], axis=0).astype(jnp.float32)
        inner_list.append(jnp.sum(cot_wide * picked, axis=1))
    inner = jnp.stack(inner_list, axis=1)
    shares = affinity / total
    affinity_grad = (route_scale / total) * (inner - jnp.sum(shares * inner, axis=1, keepdims=True))
    return mixed.astype(jnp.bfloat16), grads.astype(jnp.bfloat16), affinity_grad
```

```python
import jax
import jax.numpy as jnp
from jax import lax
from jax.experimental import pallas as pl
from jax.experimental.pallas import tpu as pltpu
from jax.sharding import PartitionSpec as P

TOP = 8
CAP = 10
FLIGHT = 32
STRIDE = 8
TOK = 256
WIDTH = 1792
FF = 1024
MAIN = 8
TAIL = 512
PACKED = WIDTH + TAIL
ROWS = FLIGHT * MAIN
HALF_MAIN = ROWS // 2
HALF = FLIGHT * CAP // 2
TILE = 256
STEPS = WIDTH // TILE
ROUTE_SCALE = 2.5
F32 = jnp.float32
BF16 = jnp.bfloat16
NN = (((1,), (0,)), ((), ()))
NT = (((1,), (1,)), ((), ()))
TN = (((0,), (0,)), ((), ()))


def dot(a, b, dims=NN, exact=False):
    precision = lax.Precision.HIGHEST if exact else None
    return lax.dot_general(a, b, dims, precision=precision, preferred_element_type=F32)


def iota(shape, dim):
    return lax.broadcasted_iota(jnp.int32, shape, dim)


def expert_marks(ids_ref, keep_ref, values_ref=None):
    expert = iota((FLIGHT, TOK), 0) * STRIDE
    marks = jnp.zeros((FLIGHT, TOK), F32)
    values = jnp.zeros((FLIGHT, TOK), F32)
    for k in range(TOP):
        hit = (ids_ref[k : k + 1, :] == expert) & (keep_ref[k : k + 1, :] == 1)
        marks = jnp.where(hit, 1.0, marks)
        if values_ref is not None:
            values = jnp.where(hit, values_ref[k : k + 1, :], values)
    return marks, values


def spread_matrix():
    return (iota((ROWS, FLIGHT), 0) // MAIN == iota((ROWS, FLIGHT), 1)).astype(F32)


def slots_spread(marks):
    earlier = (iota((TOK, TOK), 0) < iota((TOK, TOK), 1)).astype(BF16)
    position = dot(marks.astype(BF16), earlier)
    slot = jnp.where((marks > 0.5) & (position < CAP), position, 31.0)
    return dot(spread_matrix().astype(BF16), slot.astype(BF16))


def picks(marks):
    spread = slots_spread(marks)
    sub = (iota((ROWS, TOK), 0) % MAIN).astype(F32)
    tail_sub = (iota((ROWS, TOK), 0) % 2 + MAIN).astype(F32)
    return spread == sub, spread == tail_sub


def gather_into(out_ref, source_ref, main, tail, main_scale, tail_scale):
    piece_of_row = iota((ROWS, TILE), 0) % MAIN // 2
    zero = jnp.zeros((ROWS, TILE), BF16)
    tails = [zero, zero]
    for n in range(STEPS):
        block = source_ref[:, n * TILE : (n + 1) * TILE]
        first = dot(main, block)
        second = dot(tail, block)
        if main_scale is not None:
            first = first * main_scale
            second = second * tail_scale
        out_ref[:, n * TILE : (n + 1) * TILE] = first.astype(BF16)
        tails[n % 2] = jnp.where(piece_of_row == n // 2, second.astype(BF16), tails[n % 2])
    out_ref[:, WIDTH : WIDTH + TILE] = tails[0]
    out_ref[:, WIDTH + TILE :] = tails[1]


def as_bf16(mask):
    return jnp.where(mask, 1.0, 0.0).astype(BF16)


def send_tokens_kernel(ids_ref, keep_ref, source_ref, out_ref):
    marks, unused = expert_marks(ids_ref, keep_ref)
    main, tail = picks(marks)
    gather_into(out_ref, source_ref, as_bf16(main), as_bf16(tail), None, None)


def weights_of(affinity_ref):
    affinity = affinity_ref[...]
    return ROUTE_SCALE * affinity / jnp.sum(affinity, axis=0, keepdims=True)


def send_grads_kernel(ids_ref, keep_ref, affinity_ref, source_ref, out_ref, weight_ref):
    weight_ref[...] = weights_of(affinity_ref)
    marks, weights = expert_marks(ids_ref, keep_ref, weight_ref)
    main, tail = picks(marks)
    wide = dot(spread_matrix(), weights, exact=True)
    main_scale = jnp.sum(jnp.where(main, wide, 0.0), axis=1, keepdims=True)
    tail_scale = jnp.sum(jnp.where(tail, wide, 0.0), axis=1, keepdims=True)
    gather_into(out_ref, source_ref, as_bf16(main), as_bf16(tail), main_scale, tail_scale)


def vmem(n):
    return [pl.BlockSpec(memory_space=pltpu.VMEM)] * n


def cost(flops, moved):
    return pl.CostEstimate(flops=int(flops), bytes_accessed=int(moved), transcendentals=0)


GATHER_COST = cost(4 * ROWS * TOK * WIDTH, 2 * TOK * WIDTH * 3)


def send_tokens(ids, keep, source):
    return pl.pallas_call(
        send_tokens_kernel,
        out_shape=jax.ShapeDtypeStruct((ROWS, PACKED), BF16),
        in_specs=vmem(3),
        out_specs=pl.BlockSpec(memory_space=pltpu.VMEM),
        cost_estimate=GATHER_COST,
        name="send_tokens",
    )(ids, keep, source)


def send_grads(ids, keep, affinity, source):
    return pl.pallas_call(
        send_grads_kernel,
        out_shape=jax.ShapeDtypeStruct((ROWS, PACKED), BF16),
        in_specs=vmem(4),
        out_specs=pl.BlockSpec(memory_space=pltpu.VMEM),
        scratch_shapes=[pltpu.VMEM((TOP, TOK), F32)],
        cost_estimate=GATHER_COST,
        name="send_grads",
    )(ids, keep, affinity, source)


def unpack_half(packed_ref, half, out_ref, base):
    rows = pl.ds(pl.multiple_of(half * HALF_MAIN, HALF_MAIN), HALF_MAIN)
    out_ref[base : base + HALF_MAIN, :] = packed_ref[rows, :WIDTH]
    tail = packed_ref[rows, WIDTH:]
    shape = (HALF - HALF_MAIN, HALF_MAIN)
    row, col = iota(shape, 0), iota(shape, 1)
    for g in range(4):
        same = (row // 2 == col // MAIN) & (col % MAIN == 2 * g + row % 2)
        piece = dot(as_bf16(same), tail).astype(BF16)
        width = min(TAIL, WIDTH - g * TAIL)
        out_ref[base + HALF_MAIN : base + HALF, g * TAIL : g * TAIL + width] = piece[:, :width]


def partial_kernel(flipped, count, core_ref, packed_ref, *rest):
    weight_refs, (send_ref, keep_ref, rows_ref) = rest[:count], rest[count:]

    @pl.when(pl.program_id(0) == 0)
    def _():
        core = core_ref[0]
        unpack_half(packed_ref, 1 - core, rows_ref, 0)
        unpack_half(packed_ref, core, rows_ref, HALF)

    for at, weight_ref in enumerate(weight_refs):
        product = dot(rows_ref[...], weight_ref[...], NT if flipped else NN)
        cols = slice(at * TILE, (at + 1) * TILE)
        send_ref[:, cols] = product[:HALF].astype(BF16)
        keep_ref[:, cols] = product[HALF:]


def partial_sums(name, core, packed, weights, flipped):
    count = len(weights)
    wide = count * TILE
    if flipped:
        weight_spec = pl.BlockSpec((TILE, WIDTH), lambda n: (n, 0))
    else:
        weight_spec = pl.BlockSpec((WIDTH, TILE), lambda n: (0, n))
    out_spec = pl.BlockSpec((HALF, wide), lambda n: (0, n))
    return pl.pallas_call(
        lambda *refs: partial_kernel(flipped, count, *refs),
        grid=(FF // TILE,),
        out_shape=(
            jax.ShapeDtypeStruct((HALF, count * FF), BF16),
            jax.ShapeDtypeStruct((HALF, count * FF), F32),
        ),
        in_specs=[
            pl.BlockSpec(memory_space=pltpu.SMEM),
            pl.BlockSpec((ROWS, PACKED), lambda n: (0, 0)),
        ]
        + [weight_spec] * count,
        out_specs=(out_spec, out_spec),
        scratch_shapes=[pltpu.VMEM((2 * HALF, WIDTH), BF16)],
        cost_estimate=cost(4 * HALF * WIDTH * count * FF, 2 * count * FF * WIDTH),
        name=name,
    )(core, packed, *weights)


def spread_kernel(flipped, count, core_ref, own_ref, peer_ref, *rest):
    weight_refs, (out_ref,) = rest[:count], rest[count:]
    n = pl.program_id(0)
    core = core_ref[0]

    @pl.when(n == 0)
    def _():
        out_ref[:, WIDTH:] = jnp.zeros((ROWS, TAIL), BF16)

    cols = pl.ds(pl.multiple_of(n * TILE, TILE), TILE)
    tail_cols = pl.ds(pl.multiple_of(WIDTH + n % 2 * TILE, TILE), TILE)
    shape = (HALF_MAIN, HALF - HALF_MAIN)
    row, col = iota(shape, 0), iota(shape, 1)
    place = as_bf16((row // MAIN == col // 2) & (row % MAIN == n // 2 * 2 + col % 2))
    for half_ref, half in ((own_ref, core), (peer_ref, 1 - core)):
        product = jnp.zeros((HALF, TILE), F32)
        for at, weight_ref in enumerate(weight_refs):
            if flipped:
                product += dot(half_ref[:, at * FF : (at + 1) * FF], weight_ref[...], NT)
            else:
                product += dot(half_ref[:, at * FF : (at + 1) * FF], weight_ref[...])
        product = product.astype(BF16)
        rows = pl.ds(pl.multiple_of(half * HALF_MAIN, HALF_MAIN), HALF_MAIN)
        out_ref[rows, cols] = product[:HALF_MAIN]
        out_ref[rows, tail_cols] += dot(place, product[HALF_MAIN:]).astype(BF16)


def spread_rows(name, core, own, peer, weights, flipped):
    count = len(weights)
    if flipped:
        weight_spec = pl.BlockSpec((TILE, FF), lambda n: (n, 0))
    else:
        weight_spec = pl.BlockSpec((FF, TILE), lambda n: (0, n))
    half_spec = pl.BlockSpec((HALF, count * FF), lambda n: (0, 0))
    return pl.pallas_call(
        lambda *refs: spread_kernel(flipped, count, *refs),
        grid=(STEPS,),
        out_shape=jax.ShapeDtypeStruct((ROWS, PACKED), BF16),
        in_specs=[pl.BlockSpec(memory_space=pltpu.SMEM), half_spec, half_spec]
        + [weight_spec] * count,
        out_specs=pl.BlockSpec((ROWS, PACKED), lambda n: (0, 0)),
        cost_estimate=cost(4 * HALF * WIDTH * count * FF, 2 * count * FF * WIDTH),
        name=name,
    )(core, own, peer, *weights)


def add_kernel(keep_ref, recv_ref, total_ref, send_ref):
    total = keep_ref[...] + recv_ref[...].astype(F32)
    total_ref[...] = total
    send_ref[...] = total.astype(BF16)


def add_halves(name, keep, recv):
    return pl.pallas_call(
        add_kernel,
        out_shape=(
            jax.ShapeDtypeStruct(keep.shape, F32),
            jax.ShapeDtypeStruct(keep.shape, BF16),
        ),
        in_specs=vmem(2),
        out_specs=tuple(vmem(2)),
        cost_estimate=cost(keep.size, keep.size * 12),
        name=name,
    )(keep, recv)


def hidden_kernel(total_ref, recv_ref, hidden_ref):
    pre = total_ref[...] + recv_ref[...].astype(F32)
    gate, up = pre[:, :TILE], pre[:, TILE:]
    hidden_ref[...] = (gate * jax.nn.sigmoid(gate) * up).astype(BF16)


def hidden_of(total, recv):
    wide = pl.BlockSpec((HALF, 2 * TILE), lambda n: (0, n))
    return pl.pallas_call(
        hidden_kernel,
        grid=(FF // TILE,),
        out_shape=jax.ShapeDtypeStruct((HALF, FF), BF16),
        in_specs=[wide, wide],
        out_specs=pl.BlockSpec((HALF, TILE), lambda n: (0, n)),
        cost_estimate=cost(HALF * FF * 20, HALF * FF * 14),
        name="hidden",
    )(total, recv)


def pair_grad_kernel(total_ref, recv_ref, grad_total_ref, grad_recv_ref, gate_ref, up_ref):
    pre = total_ref[...] + recv_ref[...].astype(F32)
    gate, up = pre[:, :TILE], pre[:, TILE:]
    grad = grad_total_ref[...] + grad_recv_ref[...].astype(F32)
    sigma = jax.nn.sigmoid(gate)
    gate_ref[...] = (grad * up * sigma * (1.0 + gate * (1.0 - sigma))).astype(BF16)
    up_ref[...] = (grad * gate * sigma).astype(BF16)


def pair_grad_whole_kernel(total_ref, recv_ref, grad_total_ref, grad_recv_ref, out_ref):
    for n in range(FF // TILE):
        wide = slice(2 * n * TILE, 2 * (n + 1) * TILE)
        cols = slice(n * TILE, (n + 1) * TILE)
        pair_grad_kernel(
            total_ref.at[:, wide],
            recv_ref.at[:, wide],
            grad_total_ref.at[:, cols],
            grad_recv_ref.at[:, cols],
            out_ref.at[:, cols],
            out_ref.at[:, slice(FF + n * TILE, FF + (n + 1) * TILE)],
        )


def pair_grads(total, recv, grad_total, grad_recv):
    return pl.pallas_call(
        pair_grad_whole_kernel,
        out_shape=jax.ShapeDtypeStruct((HALF, 2 * FF), BF16),
        in_specs=vmem(4),
        out_specs=pl.BlockSpec(memory_space=pltpu.VMEM),
        cost_estimate=cost(HALF * FF * 30, HALF * FF * 24),
        name="pair_grads",
    )(total, recv, grad_total, grad_recv)


def mixed_kernel(ids_ref, keep_ref, affinity_ref, cot_ref, packed_ref, mixed_ref, inner_ref, weight_ref):
    weight_ref[...] = weights_of(affinity_ref)
    marks, weights = expert_marks(ids_ref, keep_ref, weight_ref)
    main, tail = picks(marks)
    wide = dot(spread_matrix(), weights, exact=True)
    piece_of_row = iota((ROWS, TOK), 0) % MAIN // 2

    def split(values):
        high = values.astype(BF16)
        return high, (values - high.astype(F32)).astype(BF16)

    main_high, main_low = split(jnp.where(main, wide, 0.0))
    found = jnp.zeros((ROWS, TOK), F32)
    tails = []
    for g in range(4):
        tails.append(split(jnp.where(tail & (piece_of_row == g), wide, 0.0)))
    main_inner = jnp.zeros((ROWS, TOK), F32)
    for n in range(STEPS):
        cols = slice(n * TILE, (n + 1) * TILE)
        g = n // 2
        cot = cot_ref[:, cols]
        rows = packed_ref[:, cols]
        tail_rows = packed_ref[:, WIDTH + n % 2 * TILE : WIDTH + (n % 2 + 1) * TILE]
        total = dot(main_high, rows, TN) + dot(main_low, rows, TN)
        total += dot(tails[g][0], tail_rows, TN) + dot(tails[g][1], tail_rows, TN)
        mixed_ref[:, cols] = total.astype(BF16)
        main_inner += dot(rows, cot, NT)
        found += jnp.where(tail & (piece_of_row == g), dot(tail_rows, cot, NT), 0.0)
    found += jnp.where(main, main_inner, 0.0)
    by_expert = dot(spread_matrix(), found, TN, exact=True)
    expert = iota((FLIGHT, TOK), 0) * STRIDE
    for k in range(TOP):
        hit = (ids_ref[k : k + 1, :] == expert) & (keep_ref[k : k + 1, :] == 1)
        inner_ref[k : k + 1, :] = jnp.sum(jnp.where(hit, by_expert, 0.0), axis=0, keepdims=True)


def mix(ids, keep, affinity, cot, packed):
    return pl.pallas_call(
        mixed_kernel,
        out_shape=(
            jax.ShapeDtypeStruct((TOK, WIDTH), BF16),
            jax.ShapeDtypeStruct((TOP, TOK), F32),
        ),
        in_specs=vmem(5),
        out_specs=tuple(vmem(2)),
        scratch_shapes=[pltpu.VMEM((TOP, TOK), F32)],
        cost_estimate=cost(12 * ROWS * TOK * WIDTH, 2 * TOK * WIDTH * 3),
        name="mix",
    )(ids, keep, affinity, cot, packed)


def token_grad_kernel(ids_ref, keep_ref, packed_ref, out_ref):
    marks, unused = expert_marks(ids_ref, keep_ref)
    main, tail = picks(marks)
    piece_of_row = iota((ROWS, TOK), 0) % MAIN // 2
    main_place = as_bf16(main)
    for n in range(STEPS):
        cols = slice(n * TILE, (n + 1) * TILE)
        tail_rows = packed_ref[:, WIDTH + n % 2 * TILE : WIDTH + (n % 2 + 1) * TILE]
        tail_place = as_bf16(tail & (piece_of_row == n // 2))
        total = dot(main_place, packed_ref[:, cols], TN) + dot(tail_place, tail_rows, TN)
        out_ref[:, cols] = total.astype(BF16)


def token_grads(ids, keep, packed):
    return pl.pallas_call(
        token_grad_kernel,
        out_shape=jax.ShapeDtypeStruct((TOK, WIDTH), BF16),
        in_specs=vmem(3),
        out_specs=pl.BlockSpec(memory_space=pltpu.VMEM),
        cost_estimate=cost(4 * ROWS * TOK * WIDTH, 2 * TOK * WIDTH * 3),
        name="token_grads",
    )(ids, keep, packed)


def exchange(packed):
    return lax.all_to_all(packed, "node", split_axis=0, concat_axis=0, tiled=True)


def swap(values, distance):
    return lax.ppermute(values, "local", [(i, i ^ distance) for i in range(4)])


def per_device(tokens, expert_ids, keep_flags, affinity, w_gate, w_up, w_down, cotangent):
    core = (lax.axis_index("local") % 2).astype(jnp.int32).reshape(1)
    ids, keep, affinity_t = expert_ids.T, keep_flags.T, affinity.T
    w_gate, w_up, w_down = w_gate[0], w_up[0], w_down[0]

    token_rows = exchange(send_tokens(ids, keep, tokens))
    grad_rows = exchange(send_grads(ids, keep, affinity_t, cotangent))

    send, own = partial_sums("pre", core, token_rows, (w_gate, w_up), False)
    total, send = add_halves("pre_add", own, swap(send, 1))
    recv = swap(send, 2)
    hidden = hidden_of(total, recv)
    out = spread_rows("rows_out", core, hidden, swap(hidden, 1), (w_down,), False)
    out = exchange(out)

    send, own = partial_sums("hidden_grad", core, grad_rows, (w_down,), True)
    grad_total, send = add_halves("grad_add", own, swap(send, 1))
    grad_recv = swap(send, 2)
    pair = pair_grads(total, recv, grad_total, grad_recv)
    back = spread_rows("rows_back", core, pair, swap(pair, 1), (w_gate, w_up), True)
    back = exchange(back)

    mixed, inner = mix(ids, keep, affinity_t, cotangent, out)
    inner = inner + swap(inner, 1)
    inner = inner + swap(inner, 2)
    scale = jnp.sum(affinity_t, axis=0, keepdims=True)
    shares = affinity_t / scale
    affinity_grad = ROUTE_SCALE / scale * (inner - jnp.sum(shares * inner, axis=0, keepdims=True))
    token_grad = token_grads(ids, keep, back)
    return mixed, token_grad, affinity_grad.T


def solution(mesh):
    placed = (
        P("node", "local"),
        P("node", None),
        P("node", None),
        P("node", None),
        P("node", "local", None),
        P("node", "local", None),
        P("node", None, "local"),
        P("node", "local"),
    )
    return jax.shard_map(
        per_device,
        mesh=mesh,
        in_specs=placed,
        out_specs=(P("node", "local"), P("node", "local"), P("node", None)),
        check_vma=False,
    )
```

```python
import jax
import jax.numpy as jnp
from jax import lax
from jax.experimental import pallas as pl
from jax.experimental.pallas import tpu as pltpu
from jax.sharding import PartitionSpec as P

TOP = 8
CAP = 10
FLIGHT = 32
STRIDE = 8
TOK = 256
WIDTH = 1792
FF = 1024
MAIN = 8
TAIL = 512
PACKED = WIDTH + TAIL
PAYLOAD = 2 * PACKED
HALF_WIDTH = WIDTH // 2
SPARE = WIDTH + 256
BLOCK = 3 * 512
ROWS = FLIGHT * MAIN
HALF_MAIN = ROWS // 2
HALF = FLIGHT * CAP // 2
TILE = 256
SPAN = 512
STEPS = WIDTH // TILE
ROUTE_SCALE = 2.5
F32 = jnp.float32
BF16 = jnp.bfloat16
NN = (((1,), (0,)), ((), ()))
NT = (((1,), (1,)), ((), ()))
TN = (((0,), (0,)), ((), ()))


def dot(a, b, dims=NN, exact=False):
    precision = lax.Precision.HIGHEST if exact else None
    return lax.dot_general(a, b, dims, precision=precision, preferred_element_type=F32)


def iota(shape, dim):
    return lax.broadcasted_iota(jnp.int32, shape, dim)


def expert_marks(ids_ref, keep_ref, values_ref=None):
    expert = iota((FLIGHT, TOK), 0) * STRIDE
    marks = jnp.zeros((FLIGHT, TOK), F32)
    values = jnp.zeros((FLIGHT, TOK), F32)
    for k in range(TOP):
        hit = (ids_ref[k : k + 1, :] == expert) & (keep_ref[k : k + 1, :] == 1)
        marks = jnp.where(hit, 1.0, marks)
        if values_ref is not None:
            values = jnp.where(hit, values_ref[k : k + 1, :], values)
    return marks, values


def spread_matrix():
    return as_bf16(iota((ROWS, FLIGHT), 0) // MAIN == iota((ROWS, FLIGHT), 1))


def slots_of(marks):
    earlier = as_bf16(iota((TOK, TOK), 0) < iota((TOK, TOK), 1))
    position = dot(marks.astype(BF16), earlier)
    return jnp.where((marks > 0.5) & (position < CAP), position, 31.0)


def picks(slot):
    spread = dot(spread_matrix(), slot.astype(BF16))
    sub = (iota((ROWS, TOK), 0) % MAIN).astype(F32)
    tail_sub = (iota((ROWS, TOK), 0) % 2 + MAIN).astype(F32)
    return spread == sub, spread == tail_sub


def as_bf16(mask):
    return jnp.where(mask, 1.0, 0.0).astype(BF16)


def halves_of(values):
    high = values.astype(BF16)
    return high, (values - high.astype(F32)).astype(BF16)


def weights_of(affinity_ref):
    affinity = affinity_ref[...]
    return ROUTE_SCALE * affinity / jnp.sum(affinity, axis=0, keepdims=True)


def send_kernel(ids_ref, keep_ref, affinity_ref, token_ref, cot_ref, out_ref, weight_ref, in_ref, packed_ref, in_sem, out_sem):
    def load(i):
        source = (token_ref, cot_ref)[i // 2]
        cols = slice(i % 2 * HALF_WIDTH, (i % 2 + 1) * HALF_WIDTH)
        return pltpu.make_async_copy(source.at[:, cols], in_ref.at[i], in_sem.at[i])

    def store(i):
        first = i // 3 * PACKED + i % 3 * HALF_WIDTH
        last = first + (TAIL if i % 3 == 2 else HALF_WIDTH)
        cols = slice(first, last)
        return pltpu.make_async_copy(packed_ref.at[:, cols], out_ref.at[:, cols], out_sem.at[i])

    for i in range(4):
        load(i).start()
    weight_ref[...] = weights_of(affinity_ref)
    marks, weights = expert_marks(ids_ref, keep_ref, weight_ref)
    main, tail = picks(slots_of(marks))
    main_place, tail_place = as_bf16(main), as_bf16(tail)
    piece_of_row = iota((ROWS, 128), 0) % MAIN // 2
    scales = None
    for array in range(2):
        if array == 1:
            high, low = halves_of(weights)
            wide = dot(spread_matrix(), high) + dot(spread_matrix(), low)
            scales = [
                jnp.sum(jnp.where(mask, wide, 0.0), axis=1, keepdims=True) for mask in (main, tail)
            ]
        tails = [jnp.zeros((ROWS, 128), BF16)] * 4
        for half in range(2):
            load(2 * array + half).wait()
            block = in_ref[2 * array + half]
            first, second = dot(main_place, block), dot(tail_place, block)
            if scales is not None:
                first, second = first * scales[0], second * scales[1]
            at = array * PACKED + half * HALF_WIDTH
            packed_ref[:, at : at + HALF_WIDTH] = first.astype(BF16)
            store(3 * array + half).start()
            second = second.astype(BF16)
            for m in range(7):
                feature = 7 * half + m
                tails[feature % 4] = jnp.where(
                    piece_of_row == feature // 4, second[:, 128 * m : 128 * (m + 1)], tails[feature % 4]
                )
        at = array * PACKED + WIDTH
        for m in range(4):
            packed_ref[:, at + 128 * m : at + 128 * (m + 1)] = tails[m]
        store(3 * array + 2).start()
    for i in range(6):
        store(i).wait()


ROOMY = pltpu.CompilerParams(vmem_limit_bytes=60 * 2**20)
LIMITED = pltpu.CompilerParams(vmem_limit_bytes=24 * 2**20)


def vmem(n):
    return [pl.BlockSpec(memory_space=pltpu.VMEM)] * n


def cost(flops, moved):
    return pl.CostEstimate(flops=int(flops), bytes_accessed=int(moved), transcendentals=0)


def send_rows(ids, keep, affinity, tokens, cotangent):
    return pl.pallas_call(
        send_kernel,
        out_shape=jax.ShapeDtypeStruct((ROWS, PAYLOAD), BF16),
        in_specs=vmem(3) + [pl.BlockSpec(memory_space=pl.ANY)] * 2,
        out_specs=pl.BlockSpec(memory_space=pl.ANY),
        scratch_shapes=[
            pltpu.VMEM((TOP, TOK), F32),
            pltpu.VMEM((4, TOK, HALF_WIDTH), BF16),
            pltpu.VMEM((ROWS, PAYLOAD), BF16),
            pltpu.SemaphoreType.DMA((4,)),
            pltpu.SemaphoreType.DMA((6,)),
        ],
        compiler_params=ROOMY,
        cost_estimate=cost(8 * ROWS * TOK * WIDTH, 2 * TOK * WIDTH * 6),
        name="send_rows",
    )(ids, keep, affinity, tokens, cotangent)


def unpack_half(packed_ref, at, half, out_ref, base):
    rows = pl.ds(pl.multiple_of(half * HALF_MAIN, HALF_MAIN), HALF_MAIN)
    out_ref[base : base + HALF_MAIN, :] = packed_ref[rows, at : at + WIDTH]
    tail = packed_ref[rows, at + WIDTH : at + PACKED]
    shape = (HALF - HALF_MAIN, HALF_MAIN)
    row, col = iota(shape, 0), iota(shape, 1)
    for g in range(4):
        same = (row // 2 == col // MAIN) & (col % MAIN == 2 * g + row % 2)
        piece = dot(as_bf16(same), tail).astype(BF16)
        width = min(TAIL, WIDTH - g * TAIL)
        out_ref[base + HALF_MAIN : base + HALF, g * TAIL : g * TAIL + width] = piece[:, :width]


def partial_kernel(flipped, spans, at, core_ref, packed_ref, *rest):
    count = len(spans)
    weight_refs, (send_ref, keep_ref, rows_ref) = rest[:count], rest[count:]
    if at is None:
        rows_ref = packed_ref
    else:
        core = core_ref[0]
        unpack_half(packed_ref, at, 1 - core, rows_ref, 0)
        unpack_half(packed_ref, at, core, rows_ref, HALF)
    for i, (weight_ref, first) in enumerate(zip(weight_refs, spans)):
        span = slice(first, first + SPAN)
        weight = weight_ref[span, :] if flipped else weight_ref[:, span]
        product = dot(rows_ref[...], weight, NT if flipped else NN)
        cols = slice(i * SPAN, (i + 1) * SPAN)
        send_ref[:, cols] = product[:HALF].astype(BF16)
        keep_ref[:, cols] = product[HALF:]


def partial_sums(name, core, packed, at, weights, spans, flipped):
    count = len(weights)
    return pl.pallas_call(
        lambda *refs: partial_kernel(flipped, spans, at, *refs),
        out_shape=(
            jax.ShapeDtypeStruct((HALF, count * SPAN), BF16),
            jax.ShapeDtypeStruct((HALF, count * SPAN), F32),
            jax.ShapeDtypeStruct((2 * HALF, WIDTH) if at is not None else (8, 128), BF16),
        ),
        in_specs=[pl.BlockSpec(memory_space=pltpu.SMEM)] + vmem(1 + count),
        out_specs=tuple(vmem(3)),
        compiler_params=LIMITED,
        cost_estimate=cost(1e6, 1e4),
        name=name,
    )(core, packed, *weights)


def grad_kernel(core_ref, packed_ref, weight_ref, send_ref, keep_ref, rows_ref):
    core = core_ref[0]
    unpack_half(packed_ref, PACKED, 1 - core, rows_ref, 0)
    unpack_half(packed_ref, PACKED, core, rows_ref, HALF)
    product = dot(rows_ref[...], weight_ref[...], NT)
    send_ref[...] = product[:HALF].astype(BF16)
    keep_ref[...] = product[HALF:]


def grad_sums(core, packed, weight):
    return pl.pallas_call(
        grad_kernel,
        out_shape=(
            jax.ShapeDtypeStruct((HALF, FF), BF16),
            jax.ShapeDtypeStruct((HALF, FF), F32),
        ),
        in_specs=[pl.BlockSpec(memory_space=pltpu.SMEM)] + vmem(2),
        out_specs=tuple(vmem(2)),
        scratch_shapes=[pltpu.VMEM((2 * HALF, WIDTH), BF16)],
        compiler_params=LIMITED,
        cost_estimate=cost(1e6, 1e4),
        name="grad",
    )(core, packed, weight)


def block_products(rows_ref, first, gate_ref, up_ref, down_ref, cols):
    span = slice(first, first + SPAN)
    out = dot(rows_ref[:, :SPAN], down_ref[span, cols])
    back = dot(rows_ref[:, SPAN : 2 * SPAN], gate_ref[cols, span], NT)
    back += dot(rows_ref[:, 2 * SPAN : BLOCK], up_ref[cols, span], NT)
    return out, back


def spread_first_kernel(own_ref, peer_ref, gate_ref, up_ref, down_ref, out_ref, back_ref, rows_ref):
    rows_ref[:HALF] = own_ref[...]
    rows_ref[HALF:] = peer_ref[...]
    for g in range(2):
        cols = slice(g * HALF_WIDTH, (g + 1) * HALF_WIDTH)
        out_ref[:, cols], back_ref[:, cols] = block_products(
            rows_ref, 0, gate_ref, up_ref, down_ref, cols
        )


def spread_first(own, peer, gate, up, down):
    return pl.pallas_call(
        spread_first_kernel,
        out_shape=(
            jax.ShapeDtypeStruct((2 * HALF, WIDTH), F32),
            jax.ShapeDtypeStruct((2 * HALF, WIDTH), F32),
        ),
        in_specs=vmem(5),
        out_specs=tuple(vmem(2)),
        scratch_shapes=[pltpu.VMEM((2 * HALF, BLOCK), BF16)],
        compiler_params=LIMITED,
        cost_estimate=cost(1e6, 1e4),
        name="spread_a",
    )(own, peer, gate, up, down)


def spread_last_kernel(core_ref, own_ref, peer_ref, gate_ref, up_ref, down_ref, out_sum, back_sum, packed_ref, rows_ref):
    core = core_ref[0]
    rows_ref[:HALF] = own_ref[:, :BLOCK]
    rows_ref[HALF:] = peer_ref[:, :BLOCK]
    for at in (WIDTH, PACKED + WIDTH):
        packed_ref[:, at : at + TAIL] = jnp.zeros((ROWS, TAIL), BF16)
    shape = (HALF_MAIN, HALF - HALF_MAIN)
    row, col = iota(shape, 0), iota(shape, 1)
    for g in range(4):
        width = min(TAIL, WIDTH - g * TAIL)
        cols = slice(g * TAIL, g * TAIL + width)
        products = block_products(rows_ref, SPAN, gate_ref, up_ref, down_ref, cols)
        place = as_bf16((row // MAIN == col // 2) & (row % MAIN == 2 * g + col % 2))
        for product, sum_ref, at in zip(products, (out_sum, back_sum), (0, PACKED)):
            product = (product + sum_ref[:, cols]).astype(BF16)
            for base, half in ((0, core), (HALF, 1 - core)):
                rows = pl.ds(pl.multiple_of(half * HALF_MAIN, HALF_MAIN), HALF_MAIN)
                packed_ref[rows, at + g * TAIL : at + g * TAIL + width] = product[
                    base : base + HALF_MAIN
                ]
                tail = dot(place, product[base + HALF_MAIN : base + HALF]).astype(BF16)
                packed_ref[rows, at + WIDTH : at + WIDTH + width] += tail
    for half_ref, half in ((own_ref, core), (peer_ref, 1 - core)):
        carried = half_ref[:, BLOCK:]
        total = jnp.zeros((HALF_MAIN, 128), F32)
        for first, count, each, base in ((0, HALF_MAIN, MAIN, 0), (HALF_MAIN, HALF - HALF_MAIN, 2, MAIN)):
            row, col = iota((HALF_MAIN, count), 0), iota((HALF_MAIN, count), 1)
            lane = iota((count, 128), 1) == base + iota((count, 128), 0) % each
            for part in range(2):
                place = as_bf16((row // MAIN == col // each) & (row % MAIN == 6 + part))
                column = carried[first : first + count, part : part + 1].astype(F32)
                total += dot(place, jnp.where(lane, column, 0.0).astype(BF16))
        rows = pl.ds(pl.multiple_of(half * HALF_MAIN, HALF_MAIN), HALF_MAIN)
        spare = slice(PACKED + SPARE, PACKED + SPARE + 128)
        packed_ref[rows, spare] = (packed_ref[rows, spare].astype(F32) + total).astype(BF16)


def spread_last(core, own, peer, gate, up, down, out_sum, back_sum):
    return pl.pallas_call(
        spread_last_kernel,
        out_shape=jax.ShapeDtypeStruct((ROWS, PAYLOAD), BF16),
        in_specs=[pl.BlockSpec(memory_space=pltpu.SMEM)] + vmem(7),
        out_specs=pl.BlockSpec(memory_space=pltpu.VMEM),
        scratch_shapes=[pltpu.VMEM((2 * HALF, BLOCK), BF16)],
        compiler_params=LIMITED,
        cost_estimate=cost(1e6, 1e4),
        name="spread_b",
    )(core, own, peer, gate, up, down, out_sum, back_sum)


def add_kernel(keep_ref, recv_ref, total_ref, send_ref):
    total = keep_ref[...] + recv_ref[...].astype(F32)
    total_ref[...] = total
    send_ref[...] = total.astype(BF16)


def add_halves(name, keep, recv):
    return pl.pallas_call(
        add_kernel,
        out_shape=(
            jax.ShapeDtypeStruct(keep.shape, F32),
            jax.ShapeDtypeStruct(keep.shape, BF16),
        ),
        in_specs=vmem(2),
        out_specs=tuple(vmem(2)),
        compiler_params=LIMITED,
        cost_estimate=cost(1e6, 1e4),
        name=name,
    )(keep, recv)


def block_kernel(first, total_ref, recv_ref, grad_total_ref, grad_recv_ref, *rest):
    pre = total_ref[...] + recv_ref[...].astype(F32)
    gate, up = pre[:, :SPAN], pre[:, SPAN:]
    cols = slice(first, first + SPAN)
    grad = grad_total_ref[:, cols] + grad_recv_ref[:, cols].astype(F32)
    sigma = jax.nn.sigmoid(gate)
    hidden = gate * sigma * up
    inner = jnp.sum(hidden * grad, axis=1, keepdims=True)
    if first == 0:
        out_ref, inner_ref = rest
        inner_ref[...] = jnp.broadcast_to(inner, (HALF, 128))
    else:
        inner_ref, out_ref = rest
        high, low = halves_of(inner + inner_ref[:, :1])
        lane = iota((HALF, 128), 1)
        both = jnp.where(lane == 0, high.astype(F32), jnp.where(lane == 1, low.astype(F32), 0.0))
        out_ref[:, BLOCK:] = both.astype(BF16)
    out_ref[:, :SPAN] = hidden.astype(BF16)
    out_ref[:, SPAN : 2 * SPAN] = (grad * up * sigma * (1.0 + gate * (1.0 - sigma))).astype(BF16)
    out_ref[:, 2 * SPAN : BLOCK] = (grad * gate * sigma).astype(BF16)


def block_of(name, first, total, recv, grad_total, grad_recv, *inner):
    block = jax.ShapeDtypeStruct((HALF, BLOCK + (128 if inner else 0)), BF16)
    return pl.pallas_call(
        lambda *refs: block_kernel(first, *refs),
        out_shape=block if inner else (block, jax.ShapeDtypeStruct((HALF, 128), F32)),
        in_specs=vmem(4 + len(inner)),
        out_specs=vmem(1)[0] if inner else tuple(vmem(2)),
        compiler_params=LIMITED,
        cost_estimate=cost(1e6, 1e4),
        name=name,
    )(total, recv, grad_total, grad_recv, *inner)


def combine_kernel(ids_ref, keep_ref, affinity_ref, packed_ref, mixed_ref, grad_ref, share_ref, weight_ref):
    weight_ref[...] = weights_of(affinity_ref)
    marks, weights = expert_marks(ids_ref, keep_ref, weight_ref)
    slot = slots_of(marks)
    main, tail = picks(slot)
    wide = dot(spread_matrix(), weights.astype(BF16))
    piece_of_row = iota((ROWS, TOK), 0) % MAIN // 2
    main_place = as_bf16(main)
    main_weight = jnp.where(main, wide, 0.0).astype(BF16)
    for n in range(STEPS):
        cols = slice(n * TILE, (n + 1) * TILE)
        chosen = tail & (piece_of_row == n // 2)
        first = WIDTH + n % 2 * TILE
        total = dot(main_weight, packed_ref[:, cols], TN)
        total += dot(
            jnp.where(chosen, wide, 0.0).astype(BF16), packed_ref[:, first : first + TILE], TN
        )
        mixed_ref[:, cols] = total.astype(BF16)
        total = dot(main_place, packed_ref[:, PACKED + n * TILE : PACKED + (n + 1) * TILE], TN)
        first += PACKED
        total += dot(as_bf16(chosen), packed_ref[:, first : first + TILE], TN)
        grad_ref[:, cols] = total.astype(BF16)

    row, col = iota((FLIGHT, ROWS), 0), iota((FLIGHT, ROWS), 1)
    both = as_bf16((col // MAIN == row) & (col % MAIN >= 6))
    carried = dot(both, packed_ref[:, PACKED + SPARE : PACKED + SPARE + 128])
    by_expert = jnp.zeros((FLIGHT, TOK), F32)
    for s in range(CAP):
        by_expert += jnp.where(slot == float(s), carried[:, s : s + 1], 0.0)
    expert = iota((FLIGHT, TOK), 0) * STRIDE
    for k in range(TOP):
        hit = (ids_ref[k : k + 1, :] == expert) & (keep_ref[k : k + 1, :] == 1)
        share_ref[k : k + 1, :] = jnp.sum(jnp.where(hit, by_expert, 0.0), axis=0, keepdims=True)
    affinity = affinity_ref[...]
    total = jnp.sum(affinity, axis=0, keepdims=True)
    inner = share_ref[...] / weight_ref[...]
    shares = affinity / total
    share_ref[...] = (
        ROUTE_SCALE / total * (inner - jnp.sum(shares * inner, axis=0, keepdims=True))
    )


def combine(ids, keep, affinity, packed):
    return pl.pallas_call(
        combine_kernel,
        out_shape=(
            jax.ShapeDtypeStruct((TOK, WIDTH), BF16),
            jax.ShapeDtypeStruct((TOK, WIDTH), BF16),
            jax.ShapeDtypeStruct((TOP, TOK), F32),
        ),
        in_specs=vmem(4),
        out_specs=tuple(vmem(3)),
        scratch_shapes=[pltpu.VMEM((TOP, TOK), F32)],
        compiler_params=LIMITED,
        cost_estimate=cost(8 * ROWS * TOK * WIDTH, 2 * TOK * WIDTH * 4),
        name="combine",
    )(ids, keep, affinity, packed)


def exchange(packed):
    return lax.all_to_all(packed, "node", split_axis=0, concat_axis=0, tiled=True)


def swap(values, distance):
    return lax.ppermute(values, "local", [(i, i ^ distance) for i in range(4)])


def per_device(tokens, expert_ids, keep_flags, affinity, w_gate, w_up, w_down, cotangent):
    core = (lax.axis_index("local") % 2).astype(jnp.int32).reshape(1)
    ids, keep, affinity_t = expert_ids.T, keep_flags.T, affinity.T
    w_gate, w_up, w_down = w_gate[0], w_up[0], w_down[0]

    rows = exchange(send_rows(ids, keep, affinity_t, tokens, cotangent))

    send_g, own_g = grad_sums(core, rows, w_down)
    total_g, send_g = add_halves("add_g", own_g, swap(send_g, 1))
    recv_g = swap(send_g, 2)
    gate_up = (w_gate, w_up)
    send_a, own_a, unpacked = partial_sums("pre_a", core, rows, 0, gate_up, (0, 0), False)
    total_a, send_a = add_halves("add_a", own_a, swap(send_a, 1))
    recv_a = swap(send_a, 2)
    unpacked, send_g = lax.optimization_barrier((unpacked, send_g))
    send_b, own_b, unused = partial_sums("pre_b", core, unpacked, None, gate_up, (SPAN, SPAN), False)
    total_b, send_b = add_halves("add_b", own_b, swap(send_b, 1))
    recv_b = swap(send_b, 2)

    block_a, inner = block_of("block_a", 0, total_a, recv_a, total_g, recv_g)
    peer_a = swap(block_a, 1)
    block_b = block_of("block_b", SPAN, total_b, recv_b, total_g, recv_g, inner)
    peer_b = swap(block_b, 1)
    block_a, block_b = lax.optimization_barrier((block_a, block_b))
    out_sum, back_sum = spread_first(block_a, peer_a, w_gate, w_up, w_down)
    payload = spread_last(core, block_b, peer_b, w_gate, w_up, w_down, out_sum, back_sum)
    rows = exchange(payload)
    mixed, token_grad, affinity_grad = combine(ids, keep, affinity_t, rows)
    return mixed, token_grad, affinity_grad.T


def solution(mesh):
    placed = (
        P("node", "local"),
        P("node", None),
        P("node", None),
        P("node", None),
        P("node", "local", None),
        P("node", "local", None),
        P("node", None, "local"),
        P("node", "local"),
    )
    return jax.shard_map(
        per_device,
        mesh=mesh,
        in_specs=placed,
        out_specs=(P("node", "local"), P("node", "local"), P("node", None)),
        check_vma=False,
    )
```

```python
import jax
import jax.numpy as jnp
from jax import lax
from jax.experimental import pallas as pl
from jax.experimental.pallas import tpu as pltpu
from jax.sharding import PartitionSpec as P

TOP = 8
CAP = 10
FLIGHT = 32
STRIDE = 8
TOK = 256
WIDTH = 1792
FF = 1024
MAIN = 8
TAIL = 512
PACKED = WIDTH + TAIL
PAYLOAD = 2 * PACKED
HALF_WIDTH = WIDTH // 2
SPARE = WIDTH + 256
BLOCK = 3 * 512
ROWS = FLIGHT * MAIN
HALF_MAIN = ROWS // 2
HALF = FLIGHT * CAP // 2
TILE = 256
SPAN = 512
STEPS = WIDTH // TILE
ROUTE_SCALE = 2.5
F32 = jnp.float32
BF16 = jnp.bfloat16
NN = (((1,), (0,)), ((), ()))
NT = (((1,), (1,)), ((), ()))
TN = (((0,), (0,)), ((), ()))


def dot(a, b, dims=NN, exact=False):
    precision = lax.Precision.HIGHEST if exact else None
    return lax.dot_general(a, b, dims, precision=precision, preferred_element_type=F32)


def iota(shape, dim):
    return lax.broadcasted_iota(jnp.int32, shape, dim)


def expert_marks(ids_ref, keep_ref, values_ref=None):
    expert = iota((FLIGHT, TOK), 0) * STRIDE
    marks = jnp.zeros((FLIGHT, TOK), F32)
    values = jnp.zeros((FLIGHT, TOK), F32)
    for k in range(TOP):
        hit = (ids_ref[k : k + 1, :] == expert) & (keep_ref[k : k + 1, :] == 1)
        marks = jnp.where(hit, 1.0, marks)
        if values_ref is not None:
            values = jnp.where(hit, values_ref[k : k + 1, :], values)
    return marks, values


def spread_matrix():
    return as_bf16(iota((ROWS, FLIGHT), 0) // MAIN == iota((ROWS, FLIGHT), 1))


def slots_of(marks):
    earlier = as_bf16(iota((TOK, TOK), 0) < iota((TOK, TOK), 1))
    position = dot(marks.astype(BF16), earlier)
    return jnp.where((marks > 0.5) & (position < CAP), position, 31.0)


def picks(slot):
    spread = dot(spread_matrix(), slot.astype(BF16))
    sub = (iota((ROWS, TOK), 0) % MAIN).astype(F32)
    tail_sub = (iota((ROWS, TOK), 0) % 2 + MAIN).astype(F32)
    return spread == sub, spread == tail_sub


def as_bf16(mask):
    return jnp.where(mask, 1.0, 0.0).astype(BF16)


def halves_of(values):
    high = values.astype(BF16)
    return high, (values - high.astype(F32)).astype(BF16)


def weights_of(affinity_ref):
    affinity = affinity_ref[...]
    return ROUTE_SCALE * affinity / jnp.sum(affinity, axis=0, keepdims=True)


def send_kernel(ids_ref, keep_ref, affinity_ref, token_ref, cot_ref, out_ref, weight_ref, in_ref, packed_ref, in_sem, out_sem):
    def load(i):
        source = (token_ref, cot_ref)[i // 2]
        cols = slice(i % 2 * HALF_WIDTH, (i % 2 + 1) * HALF_WIDTH)
        return pltpu.make_async_copy(source.at[:, cols], in_ref.at[i], in_sem.at[i])

    def store(i):
        first = i // 3 * PACKED + i % 3 * HALF_WIDTH
        last = first + (TAIL if i % 3 == 2 else HALF_WIDTH)
        cols = slice(first, last)
        return pltpu.make_async_copy(packed_ref.at[:, cols], out_ref.at[:, cols], out_sem.at[i])

    for i in range(4):
        load(i).start()
    weight_ref[...] = weights_of(affinity_ref)
    marks, weights = expert_marks(ids_ref, keep_ref, weight_ref)
    main, tail = picks(slots_of(marks))
    main_place, tail_place = as_bf16(main), as_bf16(tail)
    piece_of_row = iota((ROWS, 128), 0) % MAIN // 2
    scales = None
    for array in range(2):
        if array == 1:
            high, low = halves_of(weights)
            wide = dot(spread_matrix(), high) + dot(spread_matrix(), low)
            scales = [
                jnp.sum(jnp.where(mask, wide, 0.0), axis=1, keepdims=True) for mask in (main, tail)
            ]
        tails = [jnp.zeros((ROWS, 128), BF16)] * 4
        for half in range(2):
            load(2 * array + half).wait()
            block = in_ref[2 * array + half]
            first, second = dot(main_place, block), dot(tail_place, block)
            if scales is not None:
                first, second = first * scales[0], second * scales[1]
            at = array * PACKED + half * HALF_WIDTH
            packed_ref[:, at : at + HALF_WIDTH] = first.astype(BF16)
            store(3 * array + half).start()
            second = second.astype(BF16)
            for m in range(7):
                feature = 7 * half + m
                tails[feature % 4] = jnp.where(
                    piece_of_row == feature // 4, second[:, 128 * m : 128 * (m + 1)], tails[feature % 4]
                )
        at = array * PACKED + WIDTH
        for m in range(4):
            packed_ref[:, at + 128 * m : at + 128 * (m + 1)] = tails[m]
        store(3 * array + 2).start()
    for i in range(6):
        store(i).wait()


ROOMY = pltpu.CompilerParams(vmem_limit_bytes=60 * 2**20)
LIMITED = pltpu.CompilerParams(vmem_limit_bytes=24 * 2**20)


def vmem(n):
    return [pl.BlockSpec(memory_space=pltpu.VMEM)] * n


def cost(flops, moved):
    return pl.CostEstimate(flops=int(flops), bytes_accessed=int(moved), transcendentals=0)


def send_rows(ids, keep, affinity, tokens, cotangent):
    return pl.pallas_call(
        send_kernel,
        out_shape=jax.ShapeDtypeStruct((ROWS, PAYLOAD), BF16),
        in_specs=vmem(3) + [pl.BlockSpec(memory_space=pl.ANY)] * 2,
        out_specs=pl.BlockSpec(memory_space=pl.ANY),
        scratch_shapes=[
            pltpu.VMEM((TOP, TOK), F32),
            pltpu.VMEM((4, TOK, HALF_WIDTH), BF16),
            pltpu.VMEM((ROWS, PAYLOAD), BF16),
            pltpu.SemaphoreType.DMA((4,)),
            pltpu.SemaphoreType.DMA((6,)),
        ],
        compiler_params=ROOMY,
        cost_estimate=cost(8 * ROWS * TOK * WIDTH, 2 * TOK * WIDTH * 6),
        name="send_rows",
    )(ids, keep, affinity, tokens, cotangent)


def unpack_half(packed_ref, at, half, out_ref, base):
    rows = pl.ds(pl.multiple_of(half * HALF_MAIN, HALF_MAIN), HALF_MAIN)
    out_ref[base : base + HALF_MAIN, :] = packed_ref[rows, at : at + WIDTH]
    tail = packed_ref[rows, at + WIDTH : at + PACKED]
    shape = (HALF - HALF_MAIN, HALF_MAIN)
    row, col = iota(shape, 0), iota(shape, 1)
    for g in range(4):
        same = (row // 2 == col // MAIN) & (col % MAIN == 2 * g + row % 2)
        piece = dot(as_bf16(same), tail).astype(BF16)
        width = min(TAIL, WIDTH - g * TAIL)
        out_ref[base + HALF_MAIN : base + HALF, g * TAIL : g * TAIL + width] = piece[:, :width]


def partial_kernel(first, at, core_ref, packed_ref, gate_ref, up_ref, keep_ref, *rest):
    if at is not None:
        *send_refs, rows_ref = rest
        core = core_ref[0]
        unpack_half(packed_ref, at, 1 - core, rows_ref, 0)
        unpack_half(packed_ref, at, core, rows_ref, HALF)
    else:
        send_refs, rows_ref = rest, packed_ref
    span = slice(first, first + SPAN)
    width = 2 * SPAN // len(send_refs)
    for i, weight_ref in enumerate((gate_ref, up_ref)):
        product = dot(rows_ref[...], weight_ref[:, span])
        sent = product[:HALF].astype(BF16)
        for j in range(SPAN // width):
            send_refs[i * SPAN // width + j][...] = sent[:, j * width : (j + 1) * width]
        keep_ref[:, i * SPAN : (i + 1) * SPAN] = product[HALF:]


def partial_sums(name, core, packed, at, gate, up, first, pieces):
    shapes = (jax.ShapeDtypeStruct((HALF, 2 * SPAN), F32),)
    shapes += (jax.ShapeDtypeStruct((HALF, 2 * SPAN // pieces), BF16),) * pieces
    if at is not None:
        shapes += (jax.ShapeDtypeStruct((2 * HALF, WIDTH), BF16),)
    return pl.pallas_call(
        lambda *refs: partial_kernel(first, at, *refs),
        out_shape=shapes,
        in_specs=[pl.BlockSpec(memory_space=pltpu.SMEM)] + vmem(3),
        out_specs=tuple(vmem(len(shapes))),
        compiler_params=LIMITED,
        cost_estimate=cost(1e6, 1e4),
        name=name,
    )(core, packed, gate, up)


def grad_kernel(core_ref, packed_ref, weight_ref, send_ref, keep_ref, rows_ref):
    core = core_ref[0]
    unpack_half(packed_ref, PACKED, 1 - core, rows_ref, 0)
    unpack_half(packed_ref, PACKED, core, rows_ref, HALF)
    product = dot(rows_ref[...], weight_ref[...], NT)
    send_ref[...] = product[:HALF].astype(BF16)
    keep_ref[...] = product[HALF:]


def grad_sums(core, packed, weight):
    return pl.pallas_call(
        grad_kernel,
        out_shape=(
            jax.ShapeDtypeStruct((HALF, FF), BF16),
            jax.ShapeDtypeStruct((HALF, FF), F32),
        ),
        in_specs=[pl.BlockSpec(memory_space=pltpu.SMEM)] + vmem(2),
        out_specs=tuple(vmem(2)),
        scratch_shapes=[pltpu.VMEM((2 * HALF, WIDTH), BF16)],
        compiler_params=LIMITED,
        cost_estimate=cost(1e6, 1e4),
        name="grad",
    )(core, packed, weight)


def block_products(rows_ref, first, gate_ref, up_ref, down_ref, cols):
    span = slice(first, first + SPAN)
    out = dot(rows_ref[:, :SPAN], down_ref[span, cols])
    back = dot(rows_ref[:, SPAN : 2 * SPAN], gate_ref[cols, span], NT)
    back += dot(rows_ref[:, 2 * SPAN : BLOCK], up_ref[cols, span], NT)
    return out, back


def spread_first_kernel(*refs):
    own_refs, peer_refs = refs[:3], refs[3:6]
    gate_ref, up_ref, down_ref, out_ref, back_ref, rows_ref = refs[6:]
    for i in range(3):
        rows_ref[:HALF, i * SPAN : (i + 1) * SPAN] = own_refs[i][...]
        rows_ref[HALF:, i * SPAN : (i + 1) * SPAN] = peer_refs[i][...]
    for g in range(2):
        cols = slice(g * HALF_WIDTH, (g + 1) * HALF_WIDTH)
        out_ref[:, cols], back_ref[:, cols] = block_products(
            rows_ref, 0, gate_ref, up_ref, down_ref, cols
        )


def spread_first(own, peer, gate, up, down):
    return pl.pallas_call(
        spread_first_kernel,
        out_shape=(
            jax.ShapeDtypeStruct((2 * HALF, WIDTH), F32),
            jax.ShapeDtypeStruct((2 * HALF, WIDTH), F32),
        ),
        in_specs=vmem(9),
        out_specs=tuple(vmem(2)),
        scratch_shapes=[pltpu.VMEM((2 * HALF, BLOCK), BF16)],
        compiler_params=LIMITED,
        cost_estimate=cost(1e6, 1e4),
        name="spread_a",
    )(*own, *peer, gate, up, down)


def spread_last_kernel(core_ref, own_ref, peer_ref, gate_ref, up_ref, down_ref, out_sum, back_sum, packed_ref, rows_ref):
    core = core_ref[0]
    rows_ref[:HALF] = own_ref[:, :BLOCK]
    rows_ref[HALF:] = peer_ref[:, :BLOCK]
    for at in (WIDTH, PACKED + WIDTH):
        packed_ref[:, at : at + TAIL] = jnp.zeros((ROWS, TAIL), BF16)
    shape = (HALF_MAIN, HALF - HALF_MAIN)
    row, col = iota(shape, 0), iota(shape, 1)
    for g in range(4):
        width = min(TAIL, WIDTH - g * TAIL)
        cols = slice(g * TAIL, g * TAIL + width)
        products = block_products(rows_ref, SPAN, gate_ref, up_ref, down_ref, cols)
        place = as_bf16((row // MAIN == col // 2) & (row % MAIN == 2 * g + col % 2))
        for product, sum_ref, at in zip(products, (out_sum, back_sum), (0, PACKED)):
            product = (product + sum_ref[:, cols]).astype(BF16)
            for base, half in ((0, core), (HALF, 1 - core)):
                rows = pl.ds(pl.multiple_of(half * HALF_MAIN, HALF_MAIN), HALF_MAIN)
                packed_ref[rows, at + g * TAIL : at + g * TAIL + width] = product[
                    base : base + HALF_MAIN
                ]
                tail = dot(place, product[base + HALF_MAIN : base + HALF]).astype(BF16)
                packed_ref[rows, at + WIDTH : at + WIDTH + width] += tail
    for half_ref, half in ((own_ref, core), (peer_ref, 1 - core)):
        carried = half_ref[:, BLOCK:]
        total = jnp.zeros((HALF_MAIN, 128), F32)
        for first, count, each, base in ((0, HALF_MAIN, MAIN, 0), (HALF_MAIN, HALF - HALF_MAIN, 2, MAIN)):
            row, col = iota((HALF_MAIN, count), 0), iota((HALF_MAIN, count), 1)
            lane = iota((count, 128), 1) == base + iota((count, 128), 0) % each
            for part in range(2):
                place = as_bf16((row // MAIN == col // each) & (row % MAIN == 6 + part))
                column = carried[first : first + count, part : part + 1].astype(F32)
                total += dot(place, jnp.where(lane, column, 0.0).astype(BF16))
        rows = pl.ds(pl.multiple_of(half * HALF_MAIN, HALF_MAIN), HALF_MAIN)
        spare = slice(PACKED + SPARE, PACKED + SPARE + 128)
        packed_ref[rows, spare] = (packed_ref[rows, spare].astype(F32) + total).astype(BF16)


def spread_last(core, own, peer, gate, up, down, out_sum, back_sum):
    return pl.pallas_call(
        spread_last_kernel,
        out_shape=jax.ShapeDtypeStruct((ROWS, PAYLOAD), BF16),
        in_specs=[pl.BlockSpec(memory_space=pltpu.SMEM)] + vmem(7),
        out_specs=pl.BlockSpec(memory_space=pltpu.VMEM),
        scratch_shapes=[pltpu.VMEM((2 * HALF, BLOCK), BF16)],
        compiler_params=LIMITED,
        cost_estimate=cost(1e6, 1e4),
        name="spread_b",
    )(core, own, peer, gate, up, down, out_sum, back_sum)


def add_kernel(keep_ref, *refs):
    recv_refs, (total_ref, send_ref) = refs[:-2], refs[-2:]
    at = 0
    for recv_ref in recv_refs:
        cols = slice(at, at + recv_ref.shape[1])
        total = keep_ref[:, cols] + recv_ref[...].astype(F32)
        total_ref[:, cols] = total
        send_ref[:, cols] = total.astype(BF16)
        at += recv_ref.shape[1]


def add_halves(name, keep, *recv):
    return pl.pallas_call(
        add_kernel,
        out_shape=(
            jax.ShapeDtypeStruct(keep.shape, F32),
            jax.ShapeDtypeStruct(keep.shape, BF16),
        ),
        in_specs=vmem(1 + len(recv)),
        out_specs=tuple(vmem(2)),
        compiler_params=LIMITED,
        cost_estimate=cost(1e6, 1e4),
        name=name,
    )(keep, *recv)


def block_kernel(first, total_ref, recv_ref, grad_total_ref, grad_recv_ref, *rest):
    pre = total_ref[...] + recv_ref[...].astype(F32)
    gate, up = pre[:, :SPAN], pre[:, SPAN:]
    cols = slice(first, first + SPAN)
    grad = grad_total_ref[:, cols] + grad_recv_ref[:, cols].astype(F32)
    sigma = jax.nn.sigmoid(gate)
    hidden = gate * sigma * up
    inner = jnp.sum(hidden * grad, axis=1, keepdims=True)
    if first == 0:
        *parts, inner_ref = rest
        inner_ref[...] = jnp.broadcast_to(inner, (HALF, 128))
    else:
        inner_ref, out_ref = rest
        parts = [out_ref.at[:, i * SPAN : (i + 1) * SPAN] for i in range(3)]
        high, low = halves_of(inner + inner_ref[:, :1])
        lane = iota((HALF, 128), 1)
        both = jnp.where(lane == 0, high.astype(F32), jnp.where(lane == 1, low.astype(F32), 0.0))
        out_ref[:, BLOCK:] = both.astype(BF16)
    parts[0][...] = hidden.astype(BF16)
    parts[1][...] = (grad * up * sigma * (1.0 + gate * (1.0 - sigma))).astype(BF16)
    parts[2][...] = (grad * gate * sigma).astype(BF16)


def block_of(name, first, total, recv, grad_total, grad_recv, *inner):
    if inner:
        shapes = jax.ShapeDtypeStruct((HALF, BLOCK + 128), BF16)
    else:
        shapes = (jax.ShapeDtypeStruct((HALF, SPAN), BF16),) * 3
        shapes += (jax.ShapeDtypeStruct((HALF, 128), F32),)
    return pl.pallas_call(
        lambda *refs: block_kernel(first, *refs),
        out_shape=shapes,
        in_specs=vmem(4 + len(inner)),
        out_specs=vmem(1)[0] if inner else tuple(vmem(4)),
        compiler_params=LIMITED,
        cost_estimate=cost(1e6, 1e4),
        name=name,
    )(total, recv, grad_total, grad_recv, *inner)


def combine_kernel(ids_ref, keep_ref, affinity_ref, packed_ref, mixed_ref, grad_ref, share_ref, weight_ref):
    weight_ref[...] = weights_of(affinity_ref)
    marks, weights = expert_marks(ids_ref, keep_ref, weight_ref)
    slot = slots_of(marks)
    main, tail = picks(slot)
    wide = dot(spread_matrix(), weights.astype(BF16))
    piece_of_row = iota((ROWS, TOK), 0) % MAIN // 2
    main_place = as_bf16(main)
    main_weight = jnp.where(main, wide, 0.0).astype(BF16)
    for n in range(STEPS):
        cols = slice(n * TILE, (n + 1) * TILE)
        chosen = tail & (piece_of_row == n // 2)
        first = WIDTH + n % 2 * TILE
        total = dot(main_weight, packed_ref[:, cols], TN)
        total += dot(
            jnp.where(chosen, wide, 0.0).astype(BF16), packed_ref[:, first : first + TILE], TN
        )
        mixed_ref[:, cols] = total.astype(BF16)
        total = dot(main_place, packed_ref[:, PACKED + n * TILE : PACKED + (n + 1) * TILE], TN)
        first += PACKED
        total += dot(as_bf16(chosen), packed_ref[:, first : first + TILE], TN)
        grad_ref[:, cols] = total.astype(BF16)

    row, col = iota((FLIGHT, ROWS), 0), iota((FLIGHT, ROWS), 1)
    both = as_bf16((col // MAIN == row) & (col % MAIN >= 6))
    carried = dot(both, packed_ref[:, PACKED + SPARE : PACKED + SPARE + 128])
    by_expert = jnp.zeros((FLIGHT, TOK), F32)
    for s in range(CAP):
        by_expert += jnp.where(slot == float(s), carried[:, s : s + 1], 0.0)
    expert = iota((FLIGHT, TOK), 0) * STRIDE
    for k in range(TOP):
        hit = (ids_ref[k : k + 1, :] == expert) & (keep_ref[k : k + 1, :] == 1)
        share_ref[k : k + 1, :] = jnp.sum(jnp.where(hit, by_expert, 0.0), axis=0, keepdims=True)
    affinity = affinity_ref[...]
    total = jnp.sum(affinity, axis=0, keepdims=True)
    inner = share_ref[...] / weight_ref[...]
    shares = affinity / total
    share_ref[...] = (
        ROUTE_SCALE / total * (inner - jnp.sum(shares * inner, axis=0, keepdims=True))
    )


def combine(ids, keep, affinity, packed):
    return pl.pallas_call(
        combine_kernel,
        out_shape=(
            jax.ShapeDtypeStruct((TOK, WIDTH), BF16),
            jax.ShapeDtypeStruct((TOK, WIDTH), BF16),
            jax.ShapeDtypeStruct((TOP, TOK), F32),
        ),
        in_specs=vmem(4),
        out_specs=tuple(vmem(3)),
        scratch_shapes=[pltpu.VMEM((TOP, TOK), F32)],
        compiler_params=LIMITED,
        cost_estimate=cost(8 * ROWS * TOK * WIDTH, 2 * TOK * WIDTH * 4),
        name="combine",
    )(ids, keep, affinity, packed)


def exchange(packed):
    return lax.all_to_all(packed, "node", split_axis=0, concat_axis=0, tiled=True)


def swap(values, distance):
    return lax.ppermute(values, "local", [(i, i ^ distance) for i in range(4)])


def per_device(tokens, expert_ids, keep_flags, affinity, w_gate, w_up, w_down, cotangent):
    core = (lax.axis_index("local") % 2).astype(jnp.int32).reshape(1)
    ids, keep, affinity_t = expert_ids.T, keep_flags.T, affinity.T
    w_gate, w_up, w_down = w_gate[0], w_up[0], w_down[0]

    payload = send_rows(ids, keep, affinity_t, tokens, cotangent)
    payload, core = lax.optimization_barrier((payload, core))
    rows = exchange(payload)

    send_g, own_g = grad_sums(core, rows, w_down)
    total_g, send_g = add_halves("add_g", own_g, swap(send_g, 1))
    rows, send_g = lax.optimization_barrier((rows, send_g))
    recv_g = swap(send_g, 2)
    own_a, *sends, unpacked = partial_sums("pre_a", core, rows, 0, w_gate, w_up, 0, 4)
    total_a, send_a = add_halves("add_a", own_a, *[swap(part, 1) for part in sends])
    own_b, *sends = partial_sums("pre_b", core, unpacked, None, w_gate, w_up, SPAN, 2)
    total_b, send_b = add_halves("add_b", own_b, *[swap(part, 1) for part in sends])
    send_b, recv_g = lax.optimization_barrier((send_b, recv_g))
    recv_a = swap(send_a, 2)
    recv_b = swap(send_b, 2)

    *block_a, inner = block_of("block_a", 0, total_a, recv_a, total_g, recv_g)
    peer_a = [swap(part, 1) for part in block_a]
    out_sum, back_sum = spread_first(block_a, peer_a, w_gate, w_up, w_down)
    recv_b, out_sum, back_sum = lax.optimization_barrier((recv_b, out_sum, back_sum))
    block_b = block_of("block_b", SPAN, total_b, recv_b, total_g, recv_g, inner)
    payload = spread_last(core, block_b, swap(block_b, 1), w_gate, w_up, w_down, out_sum, back_sum)
    rows = exchange(payload)
    mixed, token_grad, affinity_grad = combine(ids, keep, affinity_t, rows)
    return mixed, token_grad, affinity_grad.T


def solution(mesh):
    placed = (
        P("node", "local"),
        P("node", None),
        P("node", None),
        P("node", None),
        P("node", "local", None),
        P("node", "local", None),
        P("node", None, "local"),
        P("node", "local"),
    )
    return jax.shard_map(
        per_device,
        mesh=mesh,
        in_specs=placed,
        out_specs=(P("node", "local"), P("node", "local"), P("node", None)),
        check_vma=False,
    )
```

```python
import jax
import jax.numpy as jnp
from jax import lax
from jax.experimental import pallas as pl
from jax.experimental.pallas import tpu as pltpu
from jax.sharding import PartitionSpec as P

TOP = 8
CAP = 10
FLIGHT = 32
STRIDE = 8
TOK = 256
WIDTH = 1792
FF = 1024
MAIN = 8
TAIL = 512
PACKED = WIDTH + TAIL
PAYLOAD = 2 * PACKED
HALF_WIDTH = WIDTH // 2
SENT = 2 * WIDTH + HALF_WIDTH
SPARE = WIDTH + 256
BLOCK = 3 * 512
ROWS = FLIGHT * MAIN
HALF_MAIN = ROWS // 2
HALF = FLIGHT * CAP // 2
TILE = 256
SPAN = 512
STEPS = WIDTH // TILE
ROUTE_SCALE = 2.5
F32 = jnp.float32
BF16 = jnp.bfloat16
NN = (((1,), (0,)), ((), ()))
NT = (((1,), (1,)), ((), ()))
TN = (((0,), (0,)), ((), ()))


def dot(a, b, dims=NN, exact=False):
    precision = lax.Precision.HIGHEST if exact else None
    return lax.dot_general(a, b, dims, precision=precision, preferred_element_type=F32)


def iota(shape, dim):
    return lax.broadcasted_iota(jnp.int32, shape, dim)


def expert_marks(ids_ref, keep_ref, values_ref=None):
    expert = iota((FLIGHT, TOK), 0) * STRIDE
    marks = jnp.zeros((FLIGHT, TOK), F32)
    values = jnp.zeros((FLIGHT, TOK), F32)
    for k in range(TOP):
        hit = (ids_ref[k : k + 1, :] == expert) & (keep_ref[k : k + 1, :] == 1)
        marks = jnp.where(hit, 1.0, marks)
        if values_ref is not None:
            values = jnp.where(hit, values_ref[k : k + 1, :], values)
    return marks, values


def spread_matrix():
    return as_bf16(iota((ROWS, FLIGHT), 0) // MAIN == iota((ROWS, FLIGHT), 1))


def slots_of(marks):
    earlier = as_bf16(iota((TOK, TOK), 0) < iota((TOK, TOK), 1))
    position = dot(marks.astype(BF16), earlier)
    return jnp.where((marks > 0.5) & (position < CAP), position, 31.0)


def picks(slot):
    spread = dot(spread_matrix(), slot.astype(BF16))
    sub = (iota((ROWS, TOK), 0) % MAIN).astype(F32)
    tail_sub = (iota((ROWS, TOK), 0) % 2 + MAIN).astype(F32)
    return spread == sub, spread == tail_sub


def as_bf16(mask):
    return jnp.where(mask, 1.0, 0.0).astype(BF16)


def halves_of(values):
    high = values.astype(BF16)
    return high, (values - high.astype(F32)).astype(BF16)


def weights_of(affinity_ref):
    affinity = affinity_ref[...]
    return ROUTE_SCALE * affinity / jnp.sum(affinity, axis=0, keepdims=True)


def send_kernel(*refs):
    route_refs, (token_ref, cot_ref, out_ref) = refs[:3], refs[3:6]
    ids_ref, keep_ref, affinity_ref, weight_ref, in_ref, packed_ref, route_sem, in_sem, out_sem = refs[6:]
    held = (ids_ref, keep_ref, affinity_ref)
    route = [pltpu.make_async_copy(route_refs[i], held[i], route_sem.at[i]) for i in range(3)]
    for copy in route:
        copy.start()

    def load(i):
        source = (token_ref, cot_ref)[i // 2]
        cols = slice(i % 2 * HALF_WIDTH, (i % 2 + 1) * HALF_WIDTH)
        return pltpu.make_async_copy(source.at[:, cols], in_ref.at[i], in_sem.at[i])

    def store(i):
        cols = slice(i * HALF_WIDTH, (i + 1) * HALF_WIDTH)
        return pltpu.make_async_copy(packed_ref.at[:, cols], out_ref.at[:, cols], out_sem.at[i])

    for i in range(4):
        load(i).start()
    for copy in route:
        copy.wait()
    weight_ref[...] = weights_of(affinity_ref)
    marks, weights = expert_marks(ids_ref, keep_ref, weight_ref)
    main, tail = picks(slots_of(marks))
    place = jnp.concatenate([as_bf16(main), as_bf16(tail)], axis=0)
    high, low = halves_of(weights)
    wide = dot(spread_matrix(), high) + dot(spread_matrix(), low)
    main_scale, tail_scale = [
        jnp.sum(jnp.where(mask, wide, 0.0), axis=1, keepdims=True) for mask in (main, tail)
    ]
    sub = iota((ROWS, HALF_WIDTH), 0) % MAIN
    tails = jnp.zeros((ROWS, HALF_WIDTH), BF16)
    for i in range(4):
        load(i).wait()
    for i in range(4):
        block = in_ref[i]
        both = dot(place, block)
        first, second = both[:ROWS], both[ROWS:]
        if i >= 2:
            first, second = first * main_scale, second * tail_scale
        packed_ref[:, i * HALF_WIDTH : (i + 1) * HALF_WIDTH] = first.astype(BF16)
        store(i).start()
        here = sub // 2 == 2 * (i % 2) + i // 2
        tails = jnp.where(here, second.astype(BF16), tails)
    packed_ref[:, 2 * WIDTH :] = tails
    store(4).start()
    for i in range(5):
        store(i).wait()


ROOMY = pltpu.CompilerParams(vmem_limit_bytes=60 * 2**20)
LIMITED = pltpu.CompilerParams(vmem_limit_bytes=24 * 2**20)


def vmem(n):
    return [pl.BlockSpec(memory_space=pltpu.VMEM)] * n


def cost(flops, moved):
    return pl.CostEstimate(flops=int(flops), bytes_accessed=int(moved), transcendentals=0)


def send_rows(ids, keep, affinity, tokens, cotangent):
    return pl.pallas_call(
        send_kernel,
        out_shape=jax.ShapeDtypeStruct((ROWS, SENT), BF16),
        in_specs=[pl.BlockSpec(memory_space=pl.ANY)] * 5,
        out_specs=pl.BlockSpec(memory_space=pl.ANY),
        scratch_shapes=[
            pltpu.VMEM((TOP, TOK), jnp.int32),
            pltpu.VMEM((TOP, TOK), jnp.int32),
            pltpu.VMEM((TOP, TOK), F32),
            pltpu.VMEM((TOP, TOK), F32),
            pltpu.VMEM((4, TOK, HALF_WIDTH), BF16),
            pltpu.VMEM((ROWS, SENT), BF16),
            pltpu.SemaphoreType.DMA((3,)),
            pltpu.SemaphoreType.DMA((4,)),
            pltpu.SemaphoreType.DMA((5,)),
        ],
        compiler_params=ROOMY,
        cost_estimate=cost(8 * ROWS * TOK * WIDTH, 2 * TOK * WIDTH * 6),
        name="send_rows",
    )(ids, keep, affinity, tokens, cotangent)


def unpack_half(packed_ref, array, half, out_ref, base):
    rows = pl.ds(pl.multiple_of(half * HALF_MAIN, HALF_MAIN), HALF_MAIN)
    out_ref[base : base + HALF_MAIN, :] = packed_ref[rows, array * WIDTH : (array + 1) * WIDTH]
    tail = packed_ref[rows, 2 * WIDTH :]
    shape = (HALF - HALF_MAIN, HALF_MAIN)
    row, col = iota(shape, 0), iota(shape, 1)
    for h in range(2):
        same = (row // 2 == col // MAIN) & (col % MAIN == 4 * h + 2 * array + row % 2)
        cols = slice(h * HALF_WIDTH, (h + 1) * HALF_WIDTH)
        out_ref[base + HALF_MAIN : base + HALF, cols] = dot(as_bf16(same), tail).astype(BF16)


def partial_kernel(first, at, core_ref, packed_ref, gate_ref, up_ref, keep_ref, *rest):
    if at is not None:
        *send_refs, rows_ref = rest
        core = core_ref[0]
        unpack_half(packed_ref, at, 1 - core, rows_ref, 0)
        unpack_half(packed_ref, at, core, rows_ref, HALF)
    else:
        send_refs, rows_ref = rest, packed_ref
    span = slice(first, first + SPAN)
    width = 2 * SPAN // len(send_refs)
    for i, weight_ref in enumerate((gate_ref, up_ref)):
        product = dot(rows_ref[...], weight_ref[:, span])
        sent = product[:HALF].astype(BF16)
        for j in range(SPAN // width):
            send_refs[i * SPAN // width + j][...] = sent[:, j * width : (j + 1) * width]
        keep_ref[:, i * SPAN : (i + 1) * SPAN] = product[HALF:]


def partial_sums(name, core, packed, at, gate, up, first, pieces):
    shapes = (jax.ShapeDtypeStruct((HALF, 2 * SPAN), F32),)
    shapes += (jax.ShapeDtypeStruct((HALF, 2 * SPAN // pieces), BF16),) * pieces
    if at is not None:
        shapes += (jax.ShapeDtypeStruct((2 * HALF, WIDTH), BF16),)
    return pl.pallas_call(
        lambda *refs: partial_kernel(first, at, *refs),
        out_shape=shapes,
        in_specs=[pl.BlockSpec(memory_space=pltpu.SMEM)] + vmem(3),
        out_specs=tuple(vmem(len(shapes))),
        compiler_params=LIMITED,
        cost_estimate=cost(1e6, 1e4),
        name=name,
    )(core, packed, gate, up)


def grad_kernel(core_ref, packed_ref, weight_ref, send_ref, keep_ref, rows_ref):
    core = core_ref[0]
    unpack_half(packed_ref, 1, 1 - core, rows_ref, 0)
    unpack_half(packed_ref, 1, core, rows_ref, HALF)
    product = dot(rows_ref[...], weight_ref[...], NT)
    send_ref[...] = product[:HALF].astype(BF16)
    keep_ref[...] = product[HALF:]


def grad_sums(core, packed, weight):
    return pl.pallas_call(
        grad_kernel,
        out_shape=(
            jax.ShapeDtypeStruct((HALF, FF), BF16),
            jax.ShapeDtypeStruct((HALF, FF), F32),
        ),
        in_specs=[pl.BlockSpec(memory_space=pltpu.SMEM)] + vmem(2),
        out_specs=tuple(vmem(2)),
        scratch_shapes=[pltpu.VMEM((2 * HALF, WIDTH), BF16)],
        compiler_params=LIMITED,
        cost_estimate=cost(1e6, 1e4),
        name="grad",
    )(core, packed, weight)


def block_products(rows_ref, first, gate_ref, up_ref, down_ref, cols):
    span = slice(first, first + SPAN)
    out = dot(rows_ref[:, :SPAN], down_ref[span, cols])
    back = dot(rows_ref[:, SPAN : 2 * SPAN], gate_ref[cols, span], NT)
    back += dot(rows_ref[:, 2 * SPAN : BLOCK], up_ref[cols, span], NT)
    return out, back


def spread_first_kernel(*refs):
    own_refs, peer_refs = refs[:3], refs[3:6]
    gate_ref, up_ref, down_ref, out_ref, back_ref, rows_ref = refs[6:]
    for i in range(3):
        rows_ref[:HALF, i * SPAN : (i + 1) * SPAN] = own_refs[i][...]
        rows_ref[HALF:, i * SPAN : (i + 1) * SPAN] = peer_refs[i][...]
    for g in range(2):
        cols = slice(g * HALF_WIDTH, (g + 1) * HALF_WIDTH)
        out_ref[:, cols], back_ref[:, cols] = block_products(
            rows_ref, 0, gate_ref, up_ref, down_ref, cols
        )


def spread_first(own, peer, gate, up, down):
    return pl.pallas_call(
        spread_first_kernel,
        out_shape=(
            jax.ShapeDtypeStruct((2 * HALF, WIDTH), F32),
            jax.ShapeDtypeStruct((2 * HALF, WIDTH), F32),
        ),
        in_specs=vmem(9),
        out_specs=tuple(vmem(2)),
        scratch_shapes=[pltpu.VMEM((2 * HALF, BLOCK), BF16)],
        compiler_params=LIMITED,
        cost_estimate=cost(1e6, 1e4),
        name="spread_a",
    )(*own, *peer, gate, up, down)


def spread_last_kernel(core_ref, own_ref, peer_ref, gate_ref, up_ref, down_ref, out_sum, back_sum, packed_ref, rows_ref):
    core = core_ref[0]
    rows_ref[:HALF] = own_ref[:, :BLOCK]
    rows_ref[HALF:] = peer_ref[:, :BLOCK]
    halves = [
        (base, pl.ds(pl.multiple_of(half * HALF_MAIN, HALF_MAIN), HALF_MAIN))
        for base, half in ((0, core), (HALF, 1 - core))
    ]
    tails = {}
    for g in range(4):
        width = min(TAIL, WIDTH - g * TAIL)
        cols = slice(g * TAIL, g * TAIL + width)
        products = block_products(rows_ref, SPAN, gate_ref, up_ref, down_ref, cols)
        for product, sum_ref, at in zip(products, (out_sum, back_sum), (0, PACKED)):
            product = (product + sum_ref[:, cols]).astype(BF16)
            for base, rows in halves:
                packed_ref[rows, at + g * TAIL : at + g * TAIL + width] = product[
                    base : base + HALF_MAIN
                ]
                tail = product[base + HALF_MAIN : base + HALF]
                if width < TAIL:
                    tail = jnp.concatenate([tail, jnp.zeros((HALF - HALF_MAIN, TAIL - width), BF16)], axis=1)
                tails[at, base, g] = tail
    row, col = iota((HALF_MAIN, HALF_MAIN), 0), iota((HALF_MAIN, HALF_MAIN), 1)
    piece, pair = col // (HALF - HALF_MAIN), col % (HALF - HALF_MAIN)
    place = as_bf16((row // MAIN == pair // 2) & (row % MAIN == 2 * piece + pair % 2))
    for at in (0, PACKED):
        for base, rows in halves:
            stacked = jnp.concatenate([tails[at, base, g] for g in range(4)], axis=0)
            packed_ref[rows, at + WIDTH : at + PACKED] = dot(place, stacked).astype(BF16)
    for half_ref, half in ((own_ref, core), (peer_ref, 1 - core)):
        carried = half_ref[:, BLOCK:]
        total = jnp.zeros((HALF_MAIN, 128), F32)
        for first, count, each, base in ((0, HALF_MAIN, MAIN, 0), (HALF_MAIN, HALF - HALF_MAIN, 2, MAIN)):
            row, col = iota((HALF_MAIN, count), 0), iota((HALF_MAIN, count), 1)
            lane = iota((count, 128), 1) == base + iota((count, 128), 0) % each
            for part in range(2):
                place = as_bf16((row // MAIN == col // each) & (row % MAIN == 6 + part))
                column = carried[first : first + count, part : part + 1].astype(F32)
                total += dot(place, jnp.where(lane, column, 0.0).astype(BF16))
        rows = pl.ds(pl.multiple_of(half * HALF_MAIN, HALF_MAIN), HALF_MAIN)
        spare = slice(PACKED + SPARE, PACKED + SPARE + 128)
        packed_ref[rows, spare] = (packed_ref[rows, spare].astype(F32) + total).astype(BF16)


def spread_last(core, own, peer, gate, up, down, out_sum, back_sum):
    return pl.pallas_call(
        spread_last_kernel,
        out_shape=jax.ShapeDtypeStruct((ROWS, PAYLOAD), BF16),
        in_specs=[pl.BlockSpec(memory_space=pltpu.SMEM)] + vmem(7),
        out_specs=pl.BlockSpec(memory_space=pltpu.VMEM),
        scratch_shapes=[pltpu.VMEM((2 * HALF, BLOCK), BF16)],
        compiler_params=LIMITED,
        cost_estimate=cost(1e6, 1e4),
        name="spread_b",
    )(core, own, peer, gate, up, down, out_sum, back_sum)


def add_kernel(keep_ref, *refs):
    recv_refs, (total_ref, send_ref) = refs[:-2], refs[-2:]
    at = 0
    for recv_ref in recv_refs:
        cols = slice(at, at + recv_ref.shape[1])
        total = keep_ref[:, cols] + recv_ref[...].astype(F32)
        total_ref[:, cols] = total
        send_ref[:, cols] = total.astype(BF16)
        at += recv_ref.shape[1]


def add_halves(name, keep, *recv):
    return pl.pallas_call(
        add_kernel,
        out_shape=(
            jax.ShapeDtypeStruct(keep.shape, F32),
            jax.ShapeDtypeStruct(keep.shape, BF16),
        ),
        in_specs=vmem(1 + len(recv)),
        out_specs=tuple(vmem(2)),
        compiler_params=LIMITED,
        cost_estimate=cost(1e6, 1e4),
        name=name,
    )(keep, *recv)


def block_kernel(first, total_ref, recv_ref, grad_total_ref, grad_recv_ref, *rest):
    pre = total_ref[...] + recv_ref[...].astype(F32)
    gate, up = pre[:, :SPAN], pre[:, SPAN:]
    cols = slice(first, first + SPAN)
    grad = grad_total_ref[:, cols] + grad_recv_ref[:, cols].astype(F32)
    sigma = jax.nn.sigmoid(gate)
    hidden = gate * sigma * up
    inner = jnp.sum(hidden * grad, axis=1, keepdims=True)
    if first == 0:
        *parts, inner_ref = rest
        inner_ref[...] = jnp.broadcast_to(inner, (HALF, 128))
    else:
        inner_ref, out_ref = rest
        parts = [out_ref.at[:, i * SPAN : (i + 1) * SPAN] for i in range(3)]
        high, low = halves_of(inner + inner_ref[:, :1])
        lane = iota((HALF, 128), 1)
        both = jnp.where(lane == 0, high.astype(F32), jnp.where(lane == 1, low.astype(F32), 0.0))
        out_ref[:, BLOCK:] = both.astype(BF16)
    parts[0][...] = hidden.astype(BF16)
    parts[1][...] = (grad * up * sigma * (1.0 + gate * (1.0 - sigma))).astype(BF16)
    parts[2][...] = (grad * gate * sigma).astype(BF16)


def block_of(name, first, total, recv, grad_total, grad_recv, *inner):
    if inner:
        shapes = jax.ShapeDtypeStruct((HALF, BLOCK + 128), BF16)
    else:
        shapes = (jax.ShapeDtypeStruct((HALF, SPAN), BF16),) * 3
        shapes += (jax.ShapeDtypeStruct((HALF, 128), F32),)
    return pl.pallas_call(
        lambda *refs: block_kernel(first, *refs),
        out_shape=shapes,
        in_specs=vmem(4 + len(inner)),
        out_specs=vmem(1)[0] if inner else tuple(vmem(4)),
        compiler_params=LIMITED,
        cost_estimate=cost(1e6, 1e4),
        name=name,
    )(total, recv, grad_total, grad_recv, *inner)


def plan_kernel(ids_ref, keep_ref, affinity_ref, places_ref, slot_ref, weight_ref):
    weight_ref[...] = weights_of(affinity_ref)
    marks, weights = expert_marks(ids_ref, keep_ref, weight_ref)
    slot = slots_of(marks)
    slot_ref[...] = slot
    wide = dot(spread_matrix(), weights.astype(BF16))
    for i, mask in enumerate(picks(slot)):
        places_ref[i] = jnp.where(mask, wide, 0.0).T.astype(BF16)
        places_ref[2 + i] = jnp.where(mask, 1.0, 0.0).T.astype(BF16)


def plan(ids, keep, affinity):
    return pl.pallas_call(
        plan_kernel,
        out_shape=(
            jax.ShapeDtypeStruct((4, TOK, ROWS), BF16),
            jax.ShapeDtypeStruct((FLIGHT, TOK), F32),
            jax.ShapeDtypeStruct((TOP, TOK), F32),
        ),
        in_specs=vmem(3),
        out_specs=tuple(vmem(3)),
        compiler_params=LIMITED,
        cost_estimate=cost(1e6, 1e4),
        name="plan",
    )(ids, keep, affinity)


def combine_kernel(ids_ref, keep_ref, affinity_ref, places_ref, slot_ref, weight_ref, packed_ref, mixed_ref, grad_ref, share_ref, held_ref, sem):
    def store(array, g):
        cols = slice(g * TAIL, min((g + 1) * TAIL, WIDTH))
        target = (mixed_ref, grad_ref)[array]
        return pltpu.make_async_copy(held_ref.at[array, :, cols], target.at[:, cols], sem.at[array, g])

    piece = iota((TOK, ROWS), 1) % MAIN // 2
    for g in range(4):
        cols = slice(g * TAIL, min((g + 1) * TAIL, WIDTH))
        width = cols.stop - cols.start
        for array in range(2):
            at = array * PACKED
            total = dot(places_ref[2 * array], packed_ref[:, at + cols.start : at + cols.stop])
            tail = places_ref[2 * array + 1]
            chosen = jnp.where(piece == g, tail, jnp.zeros_like(tail))
            total += dot(chosen, packed_ref[:, at + WIDTH : at + WIDTH + width])
            held_ref[array, :, cols] = total.astype(BF16)
            store(array, g).start()

    slot = slot_ref[...]
    row, col = iota((FLIGHT, ROWS), 0), iota((FLIGHT, ROWS), 1)
    both = as_bf16((col // MAIN == row) & (col % MAIN >= 6))
    carried = dot(both, packed_ref[:, PACKED + SPARE : PACKED + SPARE + 128])
    by_expert = jnp.zeros((FLIGHT, TOK), F32)
    for s in range(CAP):
        by_expert += jnp.where(slot == float(s), carried[:, s : s + 1], 0.0)
    expert = iota((FLIGHT, TOK), 0) * STRIDE
    for k in range(TOP):
        hit = (ids_ref[k : k + 1, :] == expert) & (keep_ref[k : k + 1, :] == 1)
        share_ref[k : k + 1, :] = jnp.sum(jnp.where(hit, by_expert, 0.0), axis=0, keepdims=True)
    affinity = affinity_ref[...]
    total = jnp.sum(affinity, axis=0, keepdims=True)
    inner = share_ref[...] / weight_ref[...]
    shares = affinity / total
    share_ref[...] = (
        ROUTE_SCALE / total * (inner - jnp.sum(shares * inner, axis=0, keepdims=True))
    )
    for array in range(2):
        for g in range(4):
            store(array, g).wait()


def combine(ids, keep, affinity, planned, packed):
    return pl.pallas_call(
        combine_kernel,
        out_shape=(
            jax.ShapeDtypeStruct((TOK, WIDTH), BF16),
            jax.ShapeDtypeStruct((TOK, WIDTH), BF16),
            jax.ShapeDtypeStruct((TOP, TOK), F32),
        ),
        in_specs=vmem(7),
        out_specs=(pl.BlockSpec(memory_space=pl.ANY),) * 2 + tuple(vmem(1)),
        scratch_shapes=[
            pltpu.VMEM((2, TOK, WIDTH), BF16),
            pltpu.SemaphoreType.DMA((2, 4)),
        ],
        compiler_params=LIMITED,
        cost_estimate=cost(8 * ROWS * TOK * WIDTH, 2 * TOK * WIDTH * 4),
        name="combine",
    )(ids, keep, affinity, *planned, packed)


def exchange(packed):
    return lax.all_to_all(packed, "node", split_axis=0, concat_axis=0, tiled=True)


def swap(values, distance):
    return lax.ppermute(values, "local", [(i, i ^ distance) for i in range(4)])


def per_device(tokens, expert_ids, keep_flags, affinity, w_gate, w_up, w_down, cotangent):
    core = (lax.axis_index("local") % 2).astype(jnp.int32).reshape(1)
    ids, keep, affinity_t = expert_ids.T, keep_flags.T, affinity.T
    w_gate, w_up, w_down = w_gate[0], w_up[0], w_down[0]

    payload = send_rows(ids, keep, affinity_t, tokens, cotangent)
    payload, core = lax.optimization_barrier((payload, core))
    rows = exchange(payload)

    send_g, own_g = grad_sums(core, rows, w_down)
    total_g, send_g = add_halves("add_g", own_g, swap(send_g, 1))
    rows, send_g = lax.optimization_barrier((rows, send_g))
    recv_g = swap(send_g, 2)
    own_a, *sends, unpacked = partial_sums("pre_a", core, rows, 0, w_gate, w_up, 0, 4)
    total_a, send_a = add_halves("add_a", own_a, *[swap(part, 1) for part in sends])
    own_b, *sends = partial_sums("pre_b", core, unpacked, None, w_gate, w_up, SPAN, 2)
    total_b, send_b = add_halves("add_b", own_b, *[swap(part, 1) for part in sends])
    send_b, recv_g = lax.optimization_barrier((send_b, recv_g))
    recv_a = swap(send_a, 2)
    route, send_b = lax.optimization_barrier(((ids, keep, affinity_t), send_b))
    recv_b = swap(send_b, 2)
    planned = plan(*route)

    *block_a, inner = block_of("block_a", 0, total_a, recv_a, total_g, recv_g)
    peer_a = [swap(part, 1) for part in block_a]
    out_sum, back_sum = spread_first(block_a, peer_a, w_gate, w_up, w_down)
    recv_b, out_sum, back_sum, planned = lax.optimization_barrier((recv_b, out_sum, back_sum, planned))
    block_b = block_of("block_b", SPAN, total_b, recv_b, total_g, recv_g, inner)
    payload = spread_last(core, block_b, swap(block_b, 1), w_gate, w_up, w_down, out_sum, back_sum)
    rows = exchange(payload)
    mixed, token_grad, affinity_grad = combine(ids, keep, affinity_t, planned, rows)
    return mixed, token_grad, affinity_grad.T


def solution(mesh):
    placed = (
        P("node", "local"),
        P("node", None),
        P("node", None),
        P("node", None),
        P("node", "local", None),
        P("node", "local", None),
        P("node", None, "local"),
        P("node", "local"),
    )
    return jax.shard_map(
        per_device,
        mesh=mesh,
        in_specs=placed,
        out_specs=(P("node", "local"), P("node", "local"), P("node", None)),
        check_vma=False,
    )
```

```python
import jax
import jax.numpy as jnp
from jax import lax
from jax.experimental import pallas as pl
from jax.experimental.pallas import tpu as pltpu
from jax.sharding import PartitionSpec as P

TOP = 8
CAP = 10
FLIGHT = 32
STRIDE = 8
TOK = 256
WIDTH = 1792
FF = 1024
MAIN = 8
TAIL = 512
PACKED = WIDTH + TAIL
PAYLOAD = 2 * PACKED
HALF_WIDTH = WIDTH // 2
SENT = 2 * WIDTH + HALF_WIDTH
SPARE = WIDTH + 256
BLOCK = 3 * 512
ROWS = FLIGHT * MAIN
HALF_MAIN = ROWS // 2
HALF = FLIGHT * CAP // 2
TILE = 256
SPAN = 512
STEPS = WIDTH // TILE
ROUTE_SCALE = 2.5
F32 = jnp.float32
BF16 = jnp.bfloat16
NN = (((1,), (0,)), ((), ()))
NT = (((1,), (1,)), ((), ()))
TN = (((0,), (0,)), ((), ()))


def dot(a, b, dims=NN, exact=False):
    precision = lax.Precision.HIGHEST if exact else None
    return lax.dot_general(a, b, dims, precision=precision, preferred_element_type=F32)


def iota(shape, dim):
    return lax.broadcasted_iota(jnp.int32, shape, dim)


def expert_marks(ids_ref, keep_ref, values_ref=None):
    expert = iota((FLIGHT, TOK), 0) * STRIDE
    marks = jnp.zeros((FLIGHT, TOK), F32)
    values = jnp.zeros((FLIGHT, TOK), F32)
    for k in range(TOP):
        hit = (ids_ref[k : k + 1, :] == expert) & (keep_ref[k : k + 1, :] == 1)
        marks = jnp.where(hit, 1.0, marks)
        if values_ref is not None:
            values = jnp.where(hit, values_ref[k : k + 1, :], values)
    return marks, values


def spread_matrix():
    return as_bf16(iota((ROWS, FLIGHT), 0) // MAIN == iota((ROWS, FLIGHT), 1))


def slots_of(marks):
    earlier = as_bf16(iota((TOK, TOK), 0) < iota((TOK, TOK), 1))
    position = dot(marks.astype(BF16), earlier)
    return jnp.where((marks > 0.5) & (position < CAP), position, 31.0)


def picks(slot):
    spread = dot(spread_matrix(), slot.astype(BF16))
    sub = (iota((ROWS, TOK), 0) % MAIN).astype(F32)
    tail_sub = (iota((ROWS, TOK), 0) % 2 + MAIN).astype(F32)
    return spread == sub, spread == tail_sub


def as_bf16(mask):
    return jnp.where(mask, 1.0, 0.0).astype(BF16)


def halves_of(values):
    high = values.astype(BF16)
    return high, (values - high.astype(F32)).astype(BF16)


def weights_of(affinity_ref):
    affinity = affinity_ref[...]
    return ROUTE_SCALE * affinity / jnp.sum(affinity, axis=0, keepdims=True)


def send_kernel(*refs):
    route_refs, (token_ref, cot_ref, out_ref) = refs[:3], refs[3:6]
    ids_ref, keep_ref, affinity_ref, weight_ref, in_ref, packed_ref, route_sem, in_sem, out_sem = refs[6:]
    held = (ids_ref, keep_ref, affinity_ref)
    route = [pltpu.make_async_copy(route_refs[i], held[i], route_sem.at[i]) for i in range(3)]
    for copy in route:
        copy.start()

    def load(i):
        source = (token_ref, cot_ref)[i // 2]
        cols = slice(i % 2 * HALF_WIDTH, (i % 2 + 1) * HALF_WIDTH)
        return pltpu.make_async_copy(source.at[:, cols], in_ref.at[i], in_sem.at[i])

    def store(i):
        cols = slice(i * HALF_WIDTH, (i + 1) * HALF_WIDTH)
        return pltpu.make_async_copy(packed_ref.at[:, cols], out_ref.at[:, cols], out_sem.at[i])

    for i in range(4):
        load(i).start()
    for copy in route:
        copy.wait()
    weight_ref[...] = weights_of(affinity_ref)
    marks, weights = expert_marks(ids_ref, keep_ref, weight_ref)
    slot = slots_of(marks)
    main, unused = picks(slot)
    dense_row = iota((2 * FLIGHT, TOK), 0)
    pair = as_bf16(iota((2 * FLIGHT, FLIGHT), 0) // 2 == iota((2 * FLIGHT, FLIGHT), 1))
    dense = dot(pair, slot.astype(BF16)) == (dense_row % 2 + MAIN).astype(F32)
    place = jnp.concatenate([as_bf16(main), as_bf16(dense)], axis=0)
    high, low = halves_of(weights)
    main_scale, tail_scale = [
        jnp.sum(jnp.where(mask, dot(copies, high) + dot(copies, low), 0.0), axis=1, keepdims=True)
        for mask, copies in ((main, spread_matrix()), (dense, pair))
    ]
    for i in range(4):
        load(i).wait()
    pieces = []
    for i in range(4):
        both = dot(place, in_ref[i])
        first, second = both[:ROWS], both[ROWS:]
        if i >= 2:
            first, second = first * main_scale, second * tail_scale
        packed_ref[:, i * HALF_WIDTH : (i + 1) * HALF_WIDTH] = first.astype(BF16)
        store(i).start()
        pieces.append(second.astype(BF16))
    row, col = iota((ROWS, ROWS), 0), iota((ROWS, ROWS), 1)
    source, expert, which = col // (2 * FLIGHT), col % (2 * FLIGHT) // 2, col % 2
    goal = 4 * (source % 2) + 2 * (source // 2) + which
    spot = as_bf16((row // MAIN == expert) & (row % MAIN == goal))
    packed_ref[:, 2 * WIDTH :] = dot(spot, jnp.concatenate(pieces, axis=0)).astype(BF16)
    store(4).start()
    for i in range(5):
        store(i).wait()


ROOMY = pltpu.CompilerParams(vmem_limit_bytes=60 * 2**20)
LIMITED = pltpu.CompilerParams(vmem_limit_bytes=24 * 2**20)


def vmem(n):
    return [pl.BlockSpec(memory_space=pltpu.VMEM)] * n


def cost(flops, moved):
    return pl.CostEstimate(flops=int(flops), bytes_accessed=int(moved), transcendentals=0)


def send_rows(ids, keep, affinity, tokens, cotangent):
    return pl.pallas_call(
        send_kernel,
        out_shape=jax.ShapeDtypeStruct((ROWS, SENT), BF16),
        in_specs=[pl.BlockSpec(memory_space=pl.ANY)] * 5,
        out_specs=pl.BlockSpec(memory_space=pl.ANY),
        scratch_shapes=[
            pltpu.VMEM((TOP, TOK), jnp.int32),
            pltpu.VMEM((TOP, TOK), jnp.int32),
            pltpu.VMEM((TOP, TOK), F32),
            pltpu.VMEM((TOP, TOK), F32),
            pltpu.VMEM((4, TOK, HALF_WIDTH), BF16),
            pltpu.VMEM((ROWS, SENT), BF16),
            pltpu.SemaphoreType.DMA((3,)),
            pltpu.SemaphoreType.DMA((4,)),
            pltpu.SemaphoreType.DMA((5,)),
        ],
        compiler_params=ROOMY,
        cost_estimate=cost(8 * ROWS * TOK * WIDTH, 2 * TOK * WIDTH * 6),
        name="send_rows",
    )(ids, keep, affinity, tokens, cotangent)


def unpack_half(packed_ref, array, half, out_ref, base):
    rows = pl.ds(pl.multiple_of(half * HALF_MAIN, HALF_MAIN), HALF_MAIN)
    out_ref[base : base + HALF_MAIN, :] = packed_ref[rows, array * WIDTH : (array + 1) * WIDTH]
    tail = packed_ref[rows, 2 * WIDTH :]
    shape = (HALF - HALF_MAIN, HALF_MAIN)
    row, col = iota(shape, 0), iota(shape, 1)
    for h in range(2):
        same = (row // 2 == col // MAIN) & (col % MAIN == 4 * h + 2 * array + row % 2)
        cols = slice(h * HALF_WIDTH, (h + 1) * HALF_WIDTH)
        out_ref[base + HALF_MAIN : base + HALF, cols] = dot(as_bf16(same), tail).astype(BF16)


def partial_kernel(first, at, core_ref, packed_ref, gate_ref, up_ref, keep_ref, *rest):
    if at is not None:
        *send_refs, rows_ref = rest
        core = core_ref[0]
        unpack_half(packed_ref, at, 1 - core, rows_ref, 0)
        unpack_half(packed_ref, at, core, rows_ref, HALF)
    else:
        send_refs, rows_ref = rest, packed_ref
    span = slice(first, first + SPAN)
    width = 2 * SPAN // len(send_refs)
    for i, weight_ref in enumerate((gate_ref, up_ref)):
        product = dot(rows_ref[...], weight_ref[:, span])
        sent = product[:HALF].astype(BF16)
        for j in range(SPAN // width):
            send_refs[i * SPAN // width + j][...] = sent[:, j * width : (j + 1) * width]
        keep_ref[:, i * SPAN : (i + 1) * SPAN] = product[HALF:]


def partial_sums(name, core, packed, at, gate, up, first, pieces):
    shapes = (jax.ShapeDtypeStruct((HALF, 2 * SPAN), F32),)
    shapes += (jax.ShapeDtypeStruct((HALF, 2 * SPAN // pieces), BF16),) * pieces
    if at is not None:
        shapes += (jax.ShapeDtypeStruct((2 * HALF, WIDTH), BF16),)
    return pl.pallas_call(
        lambda *refs: partial_kernel(first, at, *refs),
        out_shape=shapes,
        in_specs=[pl.BlockSpec(memory_space=pltpu.SMEM)] + vmem(3),
        out_specs=tuple(vmem(len(shapes))),
        compiler_params=LIMITED,
        cost_estimate=cost(1e6, 1e4),
        name=name,
    )(core, packed, gate, up)


def grad_kernel(first, core_ref, packed_ref, weight_ref, send_ref, keep_ref, *rest):
    if rest:
        rows_ref = rest[0]
        core = core_ref[0]
        unpack_half(packed_ref, 1, 1 - core, rows_ref, 0)
        unpack_half(packed_ref, 1, core, rows_ref, HALF)
    else:
        rows_ref = packed_ref
    product = dot(rows_ref[...], weight_ref[first : first + SPAN, :], NT)
    send_ref[...] = product[:HALF].astype(BF16)
    keep_ref[...] = product[HALF:]


def grad_sums(name, core, packed, weight, first):
    shapes = (
        jax.ShapeDtypeStruct((HALF, SPAN), BF16),
        jax.ShapeDtypeStruct((HALF, SPAN), F32),
    )
    if first == 0:
        shapes += (jax.ShapeDtypeStruct((2 * HALF, WIDTH), BF16),)
    return pl.pallas_call(
        lambda *refs: grad_kernel(first, *refs),
        out_shape=shapes,
        in_specs=[pl.BlockSpec(memory_space=pltpu.SMEM)] + vmem(2),
        out_specs=tuple(vmem(len(shapes))),
        compiler_params=LIMITED,
        cost_estimate=cost(1e6, 1e4),
        name=name,
    )(core, packed, weight)


def block_products(rows_ref, first, gate_ref, up_ref, down_ref, cols):
    span = slice(first, first + SPAN)
    out = dot(rows_ref[:, :SPAN], down_ref[span, cols])
    back = dot(rows_ref[:, SPAN : 2 * SPAN], gate_ref[cols, span], NT)
    back += dot(rows_ref[:, 2 * SPAN : BLOCK], up_ref[cols, span], NT)
    return out, back


def spread_first_kernel(*refs):
    own_refs, peer_refs = refs[:3], refs[3:6]
    gate_ref, up_ref, down_ref, out_ref, back_ref, rows_ref = refs[6:]
    for i in range(3):
        rows_ref[:HALF, i * SPAN : (i + 1) * SPAN] = own_refs[i][...]
        rows_ref[HALF:, i * SPAN : (i + 1) * SPAN] = peer_refs[i][...]
    for g in range(2):
        cols = slice(g * HALF_WIDTH, (g + 1) * HALF_WIDTH)
        out_ref[:, cols], back_ref[:, cols] = block_products(
            rows_ref, 0, gate_ref, up_ref, down_ref, cols
        )


def spread_first(own, peer, gate, up, down):
    return pl.pallas_call(
        spread_first_kernel,
        out_shape=(
            jax.ShapeDtypeStruct((2 * HALF, WIDTH), F32),
            jax.ShapeDtypeStruct((2 * HALF, WIDTH), F32),
        ),
        in_specs=vmem(9),
        out_specs=tuple(vmem(2)),
        scratch_shapes=[pltpu.VMEM((2 * HALF, BLOCK), BF16)],
        compiler_params=LIMITED,
        cost_estimate=cost(1e6, 1e4),
        name="spread_a",
    )(*own, *peer, gate, up, down)


def pack(core, product_of, sum_ref, packed_ref, at):
    halves = [
        (base, pl.ds(pl.multiple_of(half * HALF_MAIN, HALF_MAIN), HALF_MAIN))
        for base, half in ((0, core), (HALF, 1 - core))
    ]
    tails = {}
    for g in range(4):
        width = min(TAIL, WIDTH - g * TAIL)
        cols = slice(g * TAIL, g * TAIL + width)
        product = (product_of(cols) + sum_ref[:, cols]).astype(BF16)
        for base, rows in halves:
            packed_ref[rows, at + cols.start : at + cols.stop] = product[base : base + HALF_MAIN]
            tail = product[base + HALF_MAIN : base + HALF]
            if width < TAIL:
                rest = jnp.zeros((HALF - HALF_MAIN, TAIL - width), BF16)
                tail = jnp.concatenate([tail, rest], axis=1)
            tails[base, g] = tail
    row, col = iota((HALF_MAIN, HALF_MAIN), 0), iota((HALF_MAIN, HALF_MAIN), 1)
    piece, pair = col // (HALF - HALF_MAIN), col % (HALF - HALF_MAIN)
    place = as_bf16((row // MAIN == pair // 2) & (row % MAIN == 2 * piece + pair % 2))
    for base, rows in halves:
        stacked = jnp.concatenate([tails[base, g] for g in range(4)], axis=0)
        packed_ref[rows, at + WIDTH : at + PACKED] = dot(place, stacked).astype(BF16)


def spread_out_kernel(core_ref, *refs):
    own_refs, peer_refs, (down_ref, sum_ref, packed_ref, rows_ref) = refs[:2], refs[2:4], refs[4:]
    for i in range(2):
        rows_ref[:HALF, i * TILE : (i + 1) * TILE] = own_refs[i][...]
        rows_ref[HALF:, i * TILE : (i + 1) * TILE] = peer_refs[i][...]

    def product_of(cols):
        return dot(rows_ref[...], down_ref[SPAN:, cols])

    pack(core_ref[0], product_of, sum_ref, packed_ref, 0)


def spread_out(core, own, peer, down, out_sum):
    return pl.pallas_call(
        spread_out_kernel,
        out_shape=jax.ShapeDtypeStruct((ROWS, PACKED), BF16),
        in_specs=[pl.BlockSpec(memory_space=pltpu.SMEM)] + vmem(6),
        out_specs=pl.BlockSpec(memory_space=pltpu.VMEM),
        scratch_shapes=[pltpu.VMEM((2 * HALF, SPAN), BF16)],
        compiler_params=LIMITED,
        cost_estimate=cost(1e6, 1e4),
        name="spread_out",
    )(core, *own, *peer, down, out_sum)


def spread_last_kernel(core_ref, own_ref, peer_ref, gate_ref, up_ref, sum_ref, out_rows_ref, packed_ref, rows_ref):
    core = core_ref[0]
    rows_ref[:HALF] = own_ref[:, : 2 * SPAN]
    rows_ref[HALF:] = peer_ref[:, : 2 * SPAN]
    packed_ref[:, :PACKED] = out_rows_ref[...]

    def product_of(cols):
        product = dot(rows_ref[:, :SPAN], gate_ref[cols, SPAN:], NT)
        return product + dot(rows_ref[:, SPAN:], up_ref[cols, SPAN:], NT)

    pack(core, product_of, sum_ref, packed_ref, PACKED)
    for half_ref, half in ((own_ref, core), (peer_ref, 1 - core)):
        carried = half_ref[:, 2 * SPAN :]
        total = jnp.zeros((HALF_MAIN, 128), F32)
        for first, count, each, base in ((0, HALF_MAIN, MAIN, 0), (HALF_MAIN, HALF - HALF_MAIN, 2, MAIN)):
            row, col = iota((HALF_MAIN, count), 0), iota((HALF_MAIN, count), 1)
            lane = iota((count, 128), 1) == base + iota((count, 128), 0) % each
            for part in range(2):
                place = as_bf16((row // MAIN == col // each) & (row % MAIN == 6 + part))
                column = carried[first : first + count, part : part + 1].astype(F32)
                total += dot(place, jnp.where(lane, column, 0.0).astype(BF16))
        rows = pl.ds(pl.multiple_of(half * HALF_MAIN, HALF_MAIN), HALF_MAIN)
        spare = slice(PACKED + SPARE, PACKED + SPARE + 128)
        packed_ref[rows, spare] = (packed_ref[rows, spare].astype(F32) + total).astype(BF16)


def spread_last(core, own, peer, gate, up, back_sum, out_rows):
    return pl.pallas_call(
        spread_last_kernel,
        out_shape=jax.ShapeDtypeStruct((ROWS, PAYLOAD), BF16),
        in_specs=[pl.BlockSpec(memory_space=pltpu.SMEM)] + vmem(6),
        out_specs=pl.BlockSpec(memory_space=pltpu.VMEM),
        scratch_shapes=[pltpu.VMEM((2 * HALF, 2 * SPAN), BF16)],
        compiler_params=LIMITED,
        cost_estimate=cost(1e6, 1e4),
        name="spread_b",
    )(core, own, peer, gate, up, back_sum, out_rows)


def add_kernel(keep_ref, *refs):
    recv_refs, (total_ref, send_ref) = refs[:-2], refs[-2:]
    at = 0
    for recv_ref in recv_refs:
        cols = slice(at, at + recv_ref.shape[1])
        total = keep_ref[:, cols] + recv_ref[...].astype(F32)
        total_ref[:, cols] = total
        send_ref[:, cols] = total.astype(BF16)
        at += recv_ref.shape[1]


def add_halves(name, keep, *recv):
    return pl.pallas_call(
        add_kernel,
        out_shape=(
            jax.ShapeDtypeStruct(keep.shape, F32),
            jax.ShapeDtypeStruct(keep.shape, BF16),
        ),
        in_specs=vmem(1 + len(recv)),
        out_specs=tuple(vmem(2)),
        compiler_params=LIMITED,
        cost_estimate=cost(1e6, 1e4),
        name=name,
    )(keep, *recv)


def block_kernel(total_ref, recv_ref, grad_total_ref, grad_recv_ref, hidden_ref, gate_ref, up_ref, inner_ref):
    pre = total_ref[...] + recv_ref[...].astype(F32)
    gate, up = pre[:, :SPAN], pre[:, SPAN:]
    grad = grad_total_ref[...] + grad_recv_ref[...].astype(F32)
    sigma = jax.nn.sigmoid(gate)
    hidden = gate * sigma * up
    inner_ref[...] = jnp.broadcast_to(jnp.sum(hidden * grad, axis=1, keepdims=True), (HALF, 128))
    hidden_ref[...] = hidden.astype(BF16)
    gate_ref[...] = (grad * up * sigma * (1.0 + gate * (1.0 - sigma))).astype(BF16)
    up_ref[...] = (grad * gate * sigma).astype(BF16)


def hidden_kernel(total_ref, recv_ref, *hidden_refs):
    pre = total_ref[...] + recv_ref[...].astype(F32)
    gate, up = pre[:, :SPAN], pre[:, SPAN:]
    hidden = (gate * jax.nn.sigmoid(gate) * up).astype(BF16)
    for i, hidden_ref in enumerate(hidden_refs):
        hidden_ref[...] = hidden[:, i * TILE : (i + 1) * TILE]


def pair_kernel(total_ref, recv_ref, grad_total_ref, grad_recv_ref, inner_ref, out_ref):
    pre = total_ref[...] + recv_ref[...].astype(F32)
    gate, up = pre[:, :SPAN], pre[:, SPAN:]
    grad = grad_total_ref[...] + grad_recv_ref[...].astype(F32)
    sigma = jax.nn.sigmoid(gate)
    inner = jnp.sum(gate * sigma * up * grad, axis=1, keepdims=True)
    high, low = halves_of(inner + inner_ref[:, :1])
    lane = iota((HALF, 128), 1)
    both = jnp.where(lane == 0, high.astype(F32), jnp.where(lane == 1, low.astype(F32), 0.0))
    out_ref[:, 2 * SPAN :] = both.astype(BF16)
    out_ref[:, :SPAN] = (grad * up * sigma * (1.0 + gate * (1.0 - sigma))).astype(BF16)
    out_ref[:, SPAN : 2 * SPAN] = (grad * gate * sigma).astype(BF16)


def part_of(name, kernel, widths, *operands):
    shapes = [
        jax.ShapeDtypeStruct((HALF, width), F32 if width == 128 else BF16) for width in widths
    ]
    return pl.pallas_call(
        kernel,
        out_shape=tuple(shapes) if len(shapes) > 1 else shapes[0],
        in_specs=vmem(len(operands)),
        out_specs=tuple(vmem(len(shapes))) if len(shapes) > 1 else vmem(1)[0],
        compiler_params=LIMITED,
        cost_estimate=cost(1e6, 1e4),
        name=name,
    )(*operands)


def plan_kernel(ids_ref, keep_ref, affinity_ref, places_ref, slot_ref, weight_ref):
    weight_ref[...] = weights_of(affinity_ref)
    marks, weights = expert_marks(ids_ref, keep_ref, weight_ref)
    slot = slots_of(marks)
    slot_ref[...] = slot
    wide = dot(spread_matrix(), weights.astype(BF16))
    for i, mask in enumerate(picks(slot)):
        places_ref[i] = jnp.where(mask, wide, 0.0).T.astype(BF16)
        places_ref[2 + i] = jnp.where(mask, 1.0, 0.0).T.astype(BF16)


def plan(ids, keep, affinity):
    return pl.pallas_call(
        plan_kernel,
        out_shape=(
            jax.ShapeDtypeStruct((4, TOK, ROWS), BF16),
            jax.ShapeDtypeStruct((FLIGHT, TOK), F32),
            jax.ShapeDtypeStruct((TOP, TOK), F32),
        ),
        in_specs=vmem(3),
        out_specs=tuple(vmem(3)),
        compiler_params=LIMITED,
        cost_estimate=cost(1e6, 1e4),
        name="plan",
    )(ids, keep, affinity)


def combine_kernel(ids_ref, keep_ref, affinity_ref, places_ref, slot_ref, weight_ref, packed_ref, mixed_ref, grad_ref, share_ref, held_ref, sem):
    def store(array, g):
        cols = slice(g * TAIL, min((g + 1) * TAIL, WIDTH))
        target = (mixed_ref, grad_ref)[array]
        return pltpu.make_async_copy(held_ref.at[array, :, cols], target.at[:, cols], sem.at[array, g])

    piece = iota((TOK, ROWS), 1) % MAIN // 2
    for g in range(4):
        cols = slice(g * TAIL, min((g + 1) * TAIL, WIDTH))
        width = cols.stop - cols.start
        for array in range(2):
            at = array * PACKED
            total = dot(places_ref[2 * array], packed_ref[:, at + cols.start : at + cols.stop])
            tail = places_ref[2 * array + 1]
            chosen = jnp.where(piece == g, tail, jnp.zeros_like(tail))
            total += dot(chosen, packed_ref[:, at + WIDTH : at + WIDTH + width])
            held_ref[array, :, cols] = total.astype(BF16)
            store(array, g).start()

    slot = slot_ref[...]
    row, col = iota((FLIGHT, ROWS), 0), iota((FLIGHT, ROWS), 1)
    both = as_bf16((col // MAIN == row) & (col % MAIN >= 6))
    carried = dot(both, packed_ref[:, PACKED + SPARE : PACKED + SPARE + 128])
    by_expert = jnp.zeros((FLIGHT, TOK), F32)
    for s in range(CAP):
        by_expert += jnp.where(slot == float(s), carried[:, s : s + 1], 0.0)
    expert = iota((FLIGHT, TOK), 0) * STRIDE
    for k in range(TOP):
        hit = (ids_ref[k : k + 1, :] == expert) & (keep_ref[k : k + 1, :] == 1)
        share_ref[k : k + 1, :] = jnp.sum(jnp.where(hit, by_expert, 0.0), axis=0, keepdims=True)
    affinity = affinity_ref[...]
    total = jnp.sum(affinity, axis=0, keepdims=True)
    inner = share_ref[...] / weight_ref[...]
    shares = affinity / total
    share_ref[...] = (
        ROUTE_SCALE / total * (inner - jnp.sum(shares * inner, axis=0, keepdims=True))
    )
    for array in range(2):
        for g in range(4):
            store(array, g).wait()


def combine(ids, keep, affinity, planned, packed):
    return pl.pallas_call(
        combine_kernel,
        out_shape=(
            jax.ShapeDtypeStruct((TOK, WIDTH), BF16),
            jax.ShapeDtypeStruct((TOK, WIDTH), BF16),
            jax.ShapeDtypeStruct((TOP, TOK), F32),
        ),
        in_specs=vmem(7),
        out_specs=(pl.BlockSpec(memory_space=pl.ANY),) * 2 + tuple(vmem(1)),
        scratch_shapes=[
            pltpu.VMEM((2, TOK, WIDTH), BF16),
            pltpu.SemaphoreType.DMA((2, 4)),
        ],
        compiler_params=LIMITED,
        cost_estimate=cost(8 * ROWS * TOK * WIDTH, 2 * TOK * WIDTH * 4),
        name="combine",
    )(ids, keep, affinity, *planned, packed)


def exchange(packed):
    return lax.all_to_all(packed, "node", split_axis=0, concat_axis=0, tiled=True)


def swap(values, distance):
    return lax.ppermute(values, "local", [(i, i ^ distance) for i in range(4)])


def per_device(tokens, expert_ids, keep_flags, affinity, w_gate, w_up, w_down, cotangent):
    core = (lax.axis_index("local") % 2).astype(jnp.int32).reshape(1)
    ids, keep, affinity_t = expert_ids.T, keep_flags.T, affinity.T
    w_gate, w_up, w_down = w_gate[0], w_up[0], w_down[0]

    payload = send_rows(ids, keep, affinity_t, tokens, cotangent)
    payload, core = lax.optimization_barrier((payload, core))
    rows = exchange(payload)

    send_g, own_g, grad_rows = grad_sums("grad_a", core, rows, w_down, 0)
    total_g, send_g = add_halves("add_ga", own_g, swap(send_g, 1))
    rows, send_g = lax.optimization_barrier((rows, send_g))
    recv_g = swap(send_g, 2)
    own_a, *sends, unpacked = partial_sums("pre_a", core, rows, 0, w_gate, w_up, 0, 4)
    total_a, send_a = add_halves("add_a", own_a, *[swap(part, 1) for part in sends])
    recv_a = swap(send_a, 2)
    unpacked, recv_g = lax.optimization_barrier((unpacked, recv_g))
    own_b, *sends = partial_sums("pre_b", core, unpacked, None, w_gate, w_up, SPAN, 2)
    total_b, send_b = add_halves("add_b", own_b, *[swap(part, 1) for part in sends])
    recv_b = swap(send_b, 2)
    send_h, own_h = grad_sums("grad_b", core, grad_rows, w_down, SPAN)
    total_h, send_h = add_halves("add_gb", own_h, swap(send_h, 1))
    total_a, send_h = lax.optimization_barrier((total_a, send_h))
    recv_h = swap(send_h, 2)
    route, total_b = lax.optimization_barrier(((ids, keep, affinity_t), total_b))
    planned = plan(*route)

    *block_a, inner = part_of(
        "block_a", block_kernel, (SPAN, SPAN, SPAN, 128), total_a, recv_a, total_g, recv_g
    )
    peer_a = [swap(part, 1) for part in block_a]
    out_sum, back_sum = spread_first(block_a, peer_a, w_gate, w_up, w_down)
    recv_b, out_sum, back_sum, planned = lax.optimization_barrier((recv_b, out_sum, back_sum, planned))
    hidden_b = part_of("hidden_b", hidden_kernel, (TILE, TILE), total_b, recv_b)
    out_rows = spread_out(core, hidden_b, [swap(part, 1) for part in hidden_b], w_down, out_sum)
    recv_h, out_rows = lax.optimization_barrier((recv_h, out_rows))
    pair_b = part_of(
        "pair_b", pair_kernel, (2 * SPAN + 128,), total_b, recv_b, total_h, recv_h, inner
    )
    payload = spread_last(core, pair_b, swap(pair_b, 1), w_gate, w_up, back_sum, out_rows)
    rows = exchange(payload)
    mixed, token_grad, affinity_grad = combine(ids, keep, affinity_t, planned, rows)
    return mixed, token_grad, affinity_grad.T


def solution(mesh):
    placed = (
        P("node", "local"),
        P("node", None),
        P("node", None),
        P("node", None),
        P("node", "local", None),
        P("node", "local", None),
        P("node", None, "local"),
        P("node", "local"),
    )
    return jax.shard_map(
        per_device,
        mesh=mesh,
        in_specs=placed,
        out_specs=(P("node", "local"), P("node", "local"), P("node", None)),
        check_vma=False,
    )
```

```python
import jax
import jax.numpy as jnp
from jax import lax
from jax.experimental import pallas as pl
from jax.experimental.pallas import tpu as pltpu
from jax.sharding import PartitionSpec as P

TOP = 8
CAP = 10
FLIGHT = 32
STRIDE = 8
TOK = 256
WIDTH = 1792
FF = 1024
MAIN = 8
TAIL = 512
PACKED = WIDTH + TAIL
PAYLOAD = 2 * PACKED
HALF_WIDTH = WIDTH // 2
SENT = 2 * WIDTH + HALF_WIDTH
SPARE = WIDTH + 256
BLOCK = 3 * 512
ROWS = FLIGHT * MAIN
HALF_MAIN = ROWS // 2
HALF = FLIGHT * CAP // 2
TILE = 256
SPAN = 512
STEPS = WIDTH // TILE
ROUTE_SCALE = 2.5
F32 = jnp.float32
BF16 = jnp.bfloat16
NN = (((1,), (0,)), ((), ()))
NT = (((1,), (1,)), ((), ()))
TN = (((0,), (0,)), ((), ()))


def dot(a, b, dims=NN, exact=False):
    precision = lax.Precision.HIGHEST if exact else None
    return lax.dot_general(a, b, dims, precision=precision, preferred_element_type=F32)


def iota(shape, dim):
    return lax.broadcasted_iota(jnp.int32, shape, dim)


def expert_marks(ids_ref, keep_ref, values_ref=None):
    expert = iota((FLIGHT, TOK), 0) * STRIDE
    marks = jnp.zeros((FLIGHT, TOK), F32)
    values = jnp.zeros((FLIGHT, TOK), F32)
    for k in range(TOP):
        hit = (ids_ref[k : k + 1, :] == expert) & (keep_ref[k : k + 1, :] == 1)
        marks = jnp.where(hit, 1.0, marks)
        if values_ref is not None:
            values = jnp.where(hit, values_ref[k : k + 1, :], values)
    return marks, values


def spread_matrix():
    return as_bf16(iota((ROWS, FLIGHT), 0) // MAIN == iota((ROWS, FLIGHT), 1))


def slots_of(marks):
    earlier = as_bf16(iota((TOK, TOK), 0) < iota((TOK, TOK), 1))
    position = dot(marks.astype(BF16), earlier)
    return jnp.where((marks > 0.5) & (position < CAP), position, 31.0)


def picks(slot):
    spread = dot(spread_matrix(), slot.astype(BF16))
    sub = (iota((ROWS, TOK), 0) % MAIN).astype(F32)
    tail_sub = (iota((ROWS, TOK), 0) % 2 + MAIN).astype(F32)
    return spread == sub, spread == tail_sub


def as_bf16(mask):
    return jnp.where(mask, 1.0, 0.0).astype(BF16)


def halves_of(values):
    high = values.astype(BF16)
    return high, (values - high.astype(F32)).astype(BF16)


def weights_of(affinity_ref):
    affinity = affinity_ref[...]
    return ROUTE_SCALE * affinity / jnp.sum(affinity, axis=0, keepdims=True)


def send_kernel(*refs):
    route_refs, (token_ref, cot_ref, out_ref) = refs[:3], refs[3:6]
    ids_ref, keep_ref, affinity_ref, weight_ref, in_ref, packed_ref, route_sem, in_sem, out_sem = refs[6:]
    held = (ids_ref, keep_ref, affinity_ref)
    route = [pltpu.make_async_copy(route_refs[i], held[i], route_sem.at[i]) for i in range(3)]
    for copy in route:
        copy.start()

    def load(i):
        source = (token_ref, cot_ref)[i // 2]
        cols = slice(i % 2 * HALF_WIDTH, (i % 2 + 1) * HALF_WIDTH)
        return pltpu.make_async_copy(source.at[:, cols], in_ref.at[i], in_sem.at[i])

    def store(i):
        cols = slice(i * HALF_WIDTH, (i + 1) * HALF_WIDTH)
        return pltpu.make_async_copy(packed_ref.at[:, cols], out_ref.at[:, cols], out_sem.at[i])

    for i in range(4):
        load(i).start()
    for copy in route:
        copy.wait()
    weight_ref[...] = weights_of(affinity_ref)
    marks, weights = expert_marks(ids_ref, keep_ref, weight_ref)
    slot = slots_of(marks)
    main, unused = picks(slot)
    dense_row = iota((2 * FLIGHT, TOK), 0)
    pair = as_bf16(iota((2 * FLIGHT, FLIGHT), 0) // 2 == iota((2 * FLIGHT, FLIGHT), 1))
    dense = dot(pair, slot.astype(BF16)) == (dense_row % 2 + MAIN).astype(F32)
    place = jnp.concatenate([as_bf16(main), as_bf16(dense)], axis=0)
    high, low = halves_of(weights)
    main_scale, tail_scale = [
        jnp.sum(jnp.where(mask, dot(copies, high) + dot(copies, low), 0.0), axis=1, keepdims=True)
        for mask, copies in ((main, spread_matrix()), (dense, pair))
    ]
    for i in range(4):
        load(i).wait()
    pieces = []
    for i in range(4):
        both = dot(place, in_ref[i])
        first, second = both[:ROWS], both[ROWS:]
        if i >= 2:
            first, second = first * main_scale, second * tail_scale
        packed_ref[:, i * HALF_WIDTH : (i + 1) * HALF_WIDTH] = first.astype(BF16)
        store(i).start()
        pieces.append(second.astype(BF16))
    row, col = iota((ROWS, ROWS), 0), iota((ROWS, ROWS), 1)
    source, expert, which = col // (2 * FLIGHT), col % (2 * FLIGHT) // 2, col % 2
    goal = 4 * (source % 2) + 2 * (source // 2) + which
    spot = as_bf16((row // MAIN == expert) & (row % MAIN == goal))
    packed_ref[:, 2 * WIDTH :] = dot(spot, jnp.concatenate(pieces, axis=0)).astype(BF16)
    store(4).start()
    for i in range(5):
        store(i).wait()


ROOMY = pltpu.CompilerParams(vmem_limit_bytes=60 * 2**20)
LIMITED = pltpu.CompilerParams(vmem_limit_bytes=32 * 2**20)


def vmem(n):
    return [pl.BlockSpec(memory_space=pltpu.VMEM)] * n


def cost(flops, moved):
    return pl.CostEstimate(flops=int(flops), bytes_accessed=int(moved), transcendentals=0)


def send_rows(ids, keep, affinity, tokens, cotangent):
    return pl.pallas_call(
        send_kernel,
        out_shape=jax.ShapeDtypeStruct((ROWS, SENT), BF16),
        in_specs=[pl.BlockSpec(memory_space=pl.ANY)] * 5,
        out_specs=pl.BlockSpec(memory_space=pl.ANY),
        scratch_shapes=[
            pltpu.VMEM((TOP, TOK), jnp.int32),
            pltpu.VMEM((TOP, TOK), jnp.int32),
            pltpu.VMEM((TOP, TOK), F32),
            pltpu.VMEM((TOP, TOK), F32),
            pltpu.VMEM((4, TOK, HALF_WIDTH), BF16),
            pltpu.VMEM((ROWS, SENT), BF16),
            pltpu.SemaphoreType.DMA((3,)),
            pltpu.SemaphoreType.DMA((4,)),
            pltpu.SemaphoreType.DMA((5,)),
        ],
        compiler_params=ROOMY,
        cost_estimate=cost(8 * ROWS * TOK * WIDTH, 2 * TOK * WIDTH * 6),
        name="send_rows",
    )(ids, keep, affinity, tokens, cotangent)


def unpack_half(packed_ref, array, half, out_ref, base):
    rows = pl.ds(pl.multiple_of(half * HALF_MAIN, HALF_MAIN), HALF_MAIN)
    out_ref[base : base + HALF_MAIN, :] = packed_ref[rows, array * WIDTH : (array + 1) * WIDTH]
    tail = packed_ref[rows, 2 * WIDTH :]
    shape = (HALF - HALF_MAIN, HALF_MAIN)
    row, col = iota(shape, 0), iota(shape, 1)
    for h in range(2):
        same = (row // 2 == col // MAIN) & (col % MAIN == 4 * h + 2 * array + row % 2)
        cols = slice(h * HALF_WIDTH, (h + 1) * HALF_WIDTH)
        out_ref[base + HALF_MAIN : base + HALF, cols] = dot(as_bf16(same), tail).astype(BF16)


def partial_kernel(first, at, core_ref, packed_ref, gate_ref, up_ref, keep_ref, *rest):
    if at is not None:
        *send_refs, rows_ref = rest
        core = core_ref[0]
        unpack_half(packed_ref, at, 1 - core, rows_ref, 0)
        unpack_half(packed_ref, at, core, rows_ref, HALF)
    else:
        send_refs, rows_ref = rest, packed_ref
    span = slice(first, first + SPAN)
    sent = []
    for i, weight_ref in enumerate((gate_ref, up_ref)):
        product = dot(rows_ref[...], weight_ref[:, span])
        sent.append(product[:HALF].astype(BF16))
        keep_ref[:, i * SPAN : (i + 1) * SPAN] = product[HALF:]
    sent = jnp.concatenate(sent, axis=1)
    begin = 0
    for send_ref in send_refs:
        send_ref[...] = sent[:, begin : begin + send_ref.shape[1]]
        begin += send_ref.shape[1]


def partial_sums(name, core, packed, at, gate, up, first, pieces):
    shapes = (jax.ShapeDtypeStruct((HALF, 2 * SPAN), F32),)
    shapes += tuple(jax.ShapeDtypeStruct((HALF, width), BF16) for width in pieces)
    if at is not None:
        shapes += (jax.ShapeDtypeStruct((2 * HALF, WIDTH), BF16),)
    return pl.pallas_call(
        lambda *refs: partial_kernel(first, at, *refs),
        out_shape=shapes,
        in_specs=[pl.BlockSpec(memory_space=pltpu.SMEM)] + vmem(3),
        out_specs=tuple(vmem(len(shapes))),
        compiler_params=LIMITED,
        cost_estimate=cost(1e6, 1e4),
        name=name,
    )(core, packed, gate, up)


def grad_kernel(first, core_ref, packed_ref, weight_ref, send_ref, keep_ref, *rest):
    if rest:
        rows_ref = rest[0]
        core = core_ref[0]
        unpack_half(packed_ref, 1, 1 - core, rows_ref, 0)
        unpack_half(packed_ref, 1, core, rows_ref, HALF)
    else:
        rows_ref = packed_ref
    product = dot(rows_ref[...], weight_ref[first : first + SPAN, :], NT)
    send_ref[...] = product[:HALF].astype(BF16)
    keep_ref[...] = product[HALF:]


def grad_sums(name, core, packed, weight, first):
    shapes = (
        jax.ShapeDtypeStruct((HALF, SPAN), BF16),
        jax.ShapeDtypeStruct((HALF, SPAN), F32),
    )
    if first == 0:
        shapes += (jax.ShapeDtypeStruct((2 * HALF, WIDTH), BF16),)
    return pl.pallas_call(
        lambda *refs: grad_kernel(first, *refs),
        out_shape=shapes,
        in_specs=[pl.BlockSpec(memory_space=pltpu.SMEM)] + vmem(2),
        out_specs=tuple(vmem(len(shapes))),
        compiler_params=LIMITED,
        cost_estimate=cost(1e6, 1e4),
        name=name,
    )(core, packed, weight)


def block_products(rows_ref, first, gate_ref, up_ref, down_ref, cols):
    span = slice(first, first + SPAN)
    out = dot(rows_ref[:, :SPAN], down_ref[span, cols])
    back = dot(rows_ref[:, SPAN : 2 * SPAN], gate_ref[cols, span], NT)
    back += dot(rows_ref[:, 2 * SPAN : BLOCK], up_ref[cols, span], NT)
    return out, back


def spread_first_kernel(*refs):
    own_refs, peer_refs = refs[:3], refs[3:6]
    gate_ref, up_ref, down_ref, out_ref, back_ref, rows_ref = refs[6:]
    for i in range(3):
        rows_ref[:HALF, i * SPAN : (i + 1) * SPAN] = own_refs[i][...]
        rows_ref[HALF:, i * SPAN : (i + 1) * SPAN] = peer_refs[i][...]
    for g in range(2):
        cols = slice(g * HALF_WIDTH, (g + 1) * HALF_WIDTH)
        out_ref[:, cols], back_ref[:, cols] = block_products(
            rows_ref, 0, gate_ref, up_ref, down_ref, cols
        )


def spread_first(own, peer, gate, up, down):
    return pl.pallas_call(
        spread_first_kernel,
        out_shape=(
            jax.ShapeDtypeStruct((2 * HALF, WIDTH), F32),
            jax.ShapeDtypeStruct((2 * HALF, WIDTH), F32),
        ),
        in_specs=vmem(9),
        out_specs=tuple(vmem(2)),
        scratch_shapes=[pltpu.VMEM((2 * HALF, BLOCK), BF16)],
        compiler_params=LIMITED,
        cost_estimate=cost(1e6, 1e4),
        name="spread_a",
    )(*own, *peer, gate, up, down)


def pack(core, product_of, sum_ref, packed_ref, at):
    halves = [
        (base, pl.ds(pl.multiple_of(half * HALF_MAIN, HALF_MAIN), HALF_MAIN))
        for base, half in ((0, core), (HALF, 1 - core))
    ]
    tails = {}
    for g in range(4):
        width = min(TAIL, WIDTH - g * TAIL)
        cols = slice(g * TAIL, g * TAIL + width)
        product = (product_of(cols) + sum_ref[:, cols]).astype(BF16)
        for base, rows in halves:
            packed_ref[rows, at + cols.start : at + cols.stop] = product[base : base + HALF_MAIN]
            tail = product[base + HALF_MAIN : base + HALF]
            if width < TAIL:
                rest = jnp.zeros((HALF - HALF_MAIN, TAIL - width), BF16)
                tail = jnp.concatenate([tail, rest], axis=1)
            tails[base, g] = tail
    row, col = iota((HALF_MAIN, HALF_MAIN), 0), iota((HALF_MAIN, HALF_MAIN), 1)
    piece, pair = col // (HALF - HALF_MAIN), col % (HALF - HALF_MAIN)
    place = as_bf16((row // MAIN == pair // 2) & (row % MAIN == 2 * piece + pair % 2))
    for base, rows in halves:
        stacked = jnp.concatenate([tails[base, g] for g in range(4)], axis=0)
        packed_ref[rows, at + WIDTH : at + PACKED] = dot(place, stacked).astype(BF16)


def spread_out_kernel(core_ref, *refs):
    own_refs, peer_refs, (down_ref, sum_ref, packed_ref, rows_ref) = refs[:2], refs[2:4], refs[4:]
    for i in range(2):
        rows_ref[:HALF, i * TILE : (i + 1) * TILE] = own_refs[i][...]
        rows_ref[HALF:, i * TILE : (i + 1) * TILE] = peer_refs[i][...]

    def product_of(cols):
        return dot(rows_ref[...], down_ref[SPAN:, cols])

    pack(core_ref[0], product_of, sum_ref, packed_ref, 0)


def spread_out(core, own, peer, down, out_sum):
    return pl.pallas_call(
        spread_out_kernel,
        out_shape=jax.ShapeDtypeStruct((ROWS, PACKED), BF16),
        in_specs=[pl.BlockSpec(memory_space=pltpu.SMEM)] + vmem(6),
        out_specs=pl.BlockSpec(memory_space=pltpu.VMEM),
        scratch_shapes=[pltpu.VMEM((2 * HALF, SPAN), BF16)],
        compiler_params=LIMITED,
        cost_estimate=cost(1e6, 1e4),
        name="spread_out",
    )(core, *own, *peer, down, out_sum)


def spread_last_kernel(core_ref, own_ref, peer_ref, gate_ref, up_ref, sum_ref, out_rows_ref, packed_ref, rows_ref):
    core = core_ref[0]
    rows_ref[:HALF] = own_ref[:, : 2 * SPAN]
    rows_ref[HALF:] = peer_ref[:, : 2 * SPAN]
    packed_ref[:, :PACKED] = out_rows_ref[...]

    def product_of(cols):
        product = dot(rows_ref[:, :SPAN], gate_ref[cols, SPAN:], NT)
        return product + dot(rows_ref[:, SPAN:], up_ref[cols, SPAN:], NT)

    pack(core, product_of, sum_ref, packed_ref, PACKED)
    for half_ref, half in ((own_ref, core), (peer_ref, 1 - core)):
        carried = half_ref[:, 2 * SPAN :]
        total = jnp.zeros((HALF_MAIN, 128), F32)
        for first, count, each, base in ((0, HALF_MAIN, MAIN, 0), (HALF_MAIN, HALF - HALF_MAIN, 2, MAIN)):
            row, col = iota((HALF_MAIN, count), 0), iota((HALF_MAIN, count), 1)
            lane = iota((count, 128), 1) == base + iota((count, 128), 0) % each
            for part in range(2):
                place = as_bf16((row // MAIN == col // each) & (row % MAIN == 6 + part))
                column = carried[first : first + count, part : part + 1].astype(F32)
                total += dot(place, jnp.where(lane, column, 0.0).astype(BF16))
        rows = pl.ds(pl.multiple_of(half * HALF_MAIN, HALF_MAIN), HALF_MAIN)
        spare = slice(PACKED + SPARE, PACKED + SPARE + 128)
        packed_ref[rows, spare] = (packed_ref[rows, spare].astype(F32) + total).astype(BF16)


def spread_last(core, own, peer, gate, up, back_sum, out_rows):
    return pl.pallas_call(
        spread_last_kernel,
        out_shape=jax.ShapeDtypeStruct((ROWS, PAYLOAD), BF16),
        in_specs=[pl.BlockSpec(memory_space=pltpu.SMEM)] + vmem(6),
        out_specs=pl.BlockSpec(memory_space=pltpu.VMEM),
        scratch_shapes=[pltpu.VMEM((2 * HALF, 2 * SPAN), BF16)],
        compiler_params=LIMITED,
        cost_estimate=cost(1e6, 1e4),
        name="spread_b",
    )(core, own, peer, gate, up, back_sum, out_rows)


def add_kernel(keep_ref, *refs):
    recv_refs, (total_ref, send_ref) = refs[:-2], refs[-2:]
    at = 0
    for recv_ref in recv_refs:
        cols = slice(at, at + recv_ref.shape[1])
        total = keep_ref[:, cols] + recv_ref[...].astype(F32)
        total_ref[:, cols] = total
        send_ref[:, cols] = total.astype(BF16)
        at += recv_ref.shape[1]


def add_halves(name, keep, *recv):
    return pl.pallas_call(
        add_kernel,
        out_shape=(
            jax.ShapeDtypeStruct(keep.shape, F32),
            jax.ShapeDtypeStruct(keep.shape, BF16),
        ),
        in_specs=vmem(1 + len(recv)),
        out_specs=tuple(vmem(2)),
        compiler_params=LIMITED,
        cost_estimate=cost(1e6, 1e4),
        name=name,
    )(keep, *recv)


def block_kernel(total_ref, recv_ref, grad_total_ref, grad_recv_ref, hidden_ref, gate_ref, up_ref, inner_ref):
    pre = total_ref[...] + recv_ref[...].astype(F32)
    gate, up = pre[:, :SPAN], pre[:, SPAN:]
    grad = grad_total_ref[...] + grad_recv_ref[...].astype(F32)
    sigma = jax.nn.sigmoid(gate)
    hidden = gate * sigma * up
    inner_ref[...] = jnp.broadcast_to(jnp.sum(hidden * grad, axis=1, keepdims=True), (HALF, 128))
    hidden_ref[...] = hidden.astype(BF16)
    gate_ref[...] = (grad * up * sigma * (1.0 + gate * (1.0 - sigma))).astype(BF16)
    up_ref[...] = (grad * gate * sigma).astype(BF16)


def hidden_kernel(total_ref, recv_ref, *hidden_refs):
    pre = total_ref[...] + recv_ref[...].astype(F32)
    gate, up = pre[:, :SPAN], pre[:, SPAN:]
    hidden = (gate * jax.nn.sigmoid(gate) * up).astype(BF16)
    for i, hidden_ref in enumerate(hidden_refs):
        hidden_ref[...] = hidden[:, i * TILE : (i + 1) * TILE]


def pair_kernel(total_ref, recv_ref, grad_total_ref, grad_recv_ref, inner_ref, out_ref):
    pre = total_ref[...] + recv_ref[...].astype(F32)
    gate, up = pre[:, :SPAN], pre[:, SPAN:]
    grad = grad_total_ref[...] + grad_recv_ref[...].astype(F32)
    sigma = jax.nn.sigmoid(gate)
    inner = jnp.sum(gate * sigma * up * grad, axis=1, keepdims=True)
    high, low = halves_of(inner + inner_ref[:, :1])
    lane = iota((HALF, 128), 1)
    both = jnp.where(lane == 0, high.astype(F32), jnp.where(lane == 1, low.astype(F32), 0.0))
    out_ref[:, 2 * SPAN :] = both.astype(BF16)
    out_ref[:, :SPAN] = (grad * up * sigma * (1.0 + gate * (1.0 - sigma))).astype(BF16)
    out_ref[:, SPAN : 2 * SPAN] = (grad * gate * sigma).astype(BF16)


def part_of(name, kernel, widths, *operands):
    shapes = [
        jax.ShapeDtypeStruct((HALF, width), F32 if width == 128 else BF16) for width in widths
    ]
    return pl.pallas_call(
        kernel,
        out_shape=tuple(shapes) if len(shapes) > 1 else shapes[0],
        in_specs=vmem(len(operands)),
        out_specs=tuple(vmem(len(shapes))) if len(shapes) > 1 else vmem(1)[0],
        compiler_params=LIMITED,
        cost_estimate=cost(1e6, 1e4),
        name=name,
    )(*operands)


def plan_kernel(ids_ref, keep_ref, affinity_ref, places_ref, slot_ref, weight_ref):
    weight_ref[...] = weights_of(affinity_ref)
    marks, weights = expert_marks(ids_ref, keep_ref, weight_ref)
    slot = slots_of(marks)
    slot_ref[...] = slot
    wide = dot(spread_matrix(), weights.astype(BF16))
    for i, mask in enumerate(picks(slot)):
        places_ref[i] = jnp.where(mask, wide, 0.0).T.astype(BF16)
        places_ref[2 + i] = jnp.where(mask, 1.0, 0.0).T.astype(BF16)


def plan(ids, keep, affinity):
    return pl.pallas_call(
        plan_kernel,
        out_shape=(
            jax.ShapeDtypeStruct((4, TOK, ROWS), BF16),
            jax.ShapeDtypeStruct((FLIGHT, TOK), F32),
            jax.ShapeDtypeStruct((TOP, TOK), F32),
        ),
        in_specs=vmem(3),
        out_specs=tuple(vmem(3)),
        compiler_params=LIMITED,
        cost_estimate=cost(1e6, 1e4),
        name="plan",
    )(ids, keep, affinity)


def combine_kernel(ids_ref, keep_ref, affinity_ref, places_ref, slot_ref, weight_ref, packed_ref, mixed_ref, grad_ref, share_ref, held_ref, sem):
    def store(array, g):
        cols = slice(g * TAIL, min((g + 1) * TAIL, WIDTH))
        target = (mixed_ref, grad_ref)[array]
        return pltpu.make_async_copy(held_ref.at[array, :, cols], target.at[:, cols], sem.at[array, g])

    piece = iota((TOK, ROWS), 1) % MAIN // 2
    for g in range(4):
        cols = slice(g * TAIL, min((g + 1) * TAIL, WIDTH))
        width = cols.stop - cols.start
        for array in range(2):
            at = array * PACKED
            total = dot(places_ref[2 * array], packed_ref[:, at + cols.start : at + cols.stop])
            tail = places_ref[2 * array + 1]
            chosen = jnp.where(piece == g, tail, jnp.zeros_like(tail))
            total += dot(chosen, packed_ref[:, at + WIDTH : at + WIDTH + width])
            held_ref[array, :, cols] = total.astype(BF16)
            store(array, g).start()

    slot = slot_ref[...]
    row, col = iota((FLIGHT, ROWS), 0), iota((FLIGHT, ROWS), 1)
    both = as_bf16((col // MAIN == row) & (col % MAIN >= 6))
    carried = dot(both, packed_ref[:, PACKED + SPARE : PACKED + SPARE + 128])
    by_expert = jnp.zeros((FLIGHT, TOK), F32)
    for s in range(CAP):
        by_expert += jnp.where(slot == float(s), carried[:, s : s + 1], 0.0)
    expert = iota((FLIGHT, TOK), 0) * STRIDE
    for k in range(TOP):
        hit = (ids_ref[k : k + 1, :] == expert) & (keep_ref[k : k + 1, :] == 1)
        share_ref[k : k + 1, :] = jnp.sum(jnp.where(hit, by_expert, 0.0), axis=0, keepdims=True)
    affinity = affinity_ref[...]
    total = jnp.sum(affinity, axis=0, keepdims=True)
    inner = share_ref[...] / weight_ref[...]
    shares = affinity / total
    share_ref[...] = (
        ROUTE_SCALE / total * (inner - jnp.sum(shares * inner, axis=0, keepdims=True))
    )
    for array in range(2):
        for g in range(4):
            store(array, g).wait()


def combine(ids, keep, affinity, planned, packed):
    return pl.pallas_call(
        combine_kernel,
        out_shape=(
            jax.ShapeDtypeStruct((TOK, WIDTH), BF16),
            jax.ShapeDtypeStruct((TOK, WIDTH), BF16),
            jax.ShapeDtypeStruct((TOP, TOK), F32),
        ),
        in_specs=vmem(7),
        out_specs=(pl.BlockSpec(memory_space=pl.ANY),) * 2 + tuple(vmem(1)),
        scratch_shapes=[
            pltpu.VMEM((2, TOK, WIDTH), BF16),
            pltpu.SemaphoreType.DMA((2, 4)),
        ],
        compiler_params=LIMITED,
        cost_estimate=cost(8 * ROWS * TOK * WIDTH, 2 * TOK * WIDTH * 4),
        name="combine",
    )(ids, keep, affinity, *planned, packed)


def exchange(packed):
    return lax.all_to_all(packed, "node", split_axis=0, concat_axis=0, tiled=True)


def swap(values, distance):
    return lax.ppermute(values, "local", [(i, i ^ distance) for i in range(4)])


def per_device(tokens, expert_ids, keep_flags, affinity, w_gate, w_up, w_down, cotangent):
    core = (lax.axis_index("local") % 2).astype(jnp.int32).reshape(1)
    ids, keep, affinity_t = expert_ids.T, keep_flags.T, affinity.T
    w_gate, w_up, w_down = w_gate[0], w_up[0], w_down[0]

    payload = send_rows(ids, keep, affinity_t, tokens, cotangent)
    payload, core = lax.optimization_barrier((payload, core))
    rows = exchange(payload)

    send_g, own_g, grad_rows = grad_sums("grad_a", core, rows, w_down, 0)
    total_g, send_g = add_halves("add_ga", own_g, swap(send_g, 1))
    rows, send_g = lax.optimization_barrier((rows, send_g))
    recv_g = swap(send_g, 2)
    own_a, *sends, unpacked = partial_sums("pre_a", core, rows, 0, w_gate, w_up, 0, (384, 384, 256))
    total_a, send_a = add_halves("add_a", own_a, *[swap(part, 1) for part in sends])
    recv_a = swap(send_a, 2)
    unpacked, recv_g = lax.optimization_barrier((unpacked, recv_g))
    own_b, *sends = partial_sums("pre_b", core, unpacked, None, w_gate, w_up, SPAN, (SPAN, SPAN))
    total_b, send_b = add_halves("add_b", own_b, *[swap(part, 1) for part in sends])
    recv_b = swap(send_b, 2)
    send_h, own_h = grad_sums("grad_b", core, grad_rows, w_down, SPAN)
    total_h, send_h = add_halves("add_gb", own_h, swap(send_h, 1))
    total_a, send_h = lax.optimization_barrier((total_a, send_h))
    recv_h = swap(send_h, 2)
    route, total_b = lax.optimization_barrier(((ids, keep, affinity_t), total_b))
    planned = plan(*route)

    *block_a, inner = part_of(
        "block_a", block_kernel, (SPAN, SPAN, SPAN, 128), total_a, recv_a, total_g, recv_g
    )
    peer_a = [swap(part, 1) for part in block_a]
    out_sum, back_sum = spread_first(block_a, peer_a, w_gate, w_up, w_down)
    recv_b, out_sum, back_sum, planned = lax.optimization_barrier((recv_b, out_sum, back_sum, planned))
    hidden_b = part_of("hidden_b", hidden_kernel, (TILE, TILE), total_b, recv_b)
    out_rows = spread_out(core, hidden_b, [swap(part, 1) for part in hidden_b], w_down, out_sum)
    recv_h, out_rows = lax.optimization_barrier((recv_h, out_rows))
    pair_b = part_of(
        "pair_b", pair_kernel, (2 * SPAN + 128,), total_b, recv_b, total_h, recv_h, inner
    )
    payload = spread_last(core, pair_b, swap(pair_b, 1), w_gate, w_up, back_sum, out_rows)
    rows = exchange(payload)
    mixed, token_grad, affinity_grad = combine(ids, keep, affinity_t, planned, rows)
    return mixed, token_grad, affinity_grad.T


def solution(mesh):
    placed = (
        P("node", "local"),
        P("node", None),
        P("node", None),
        P("node", None),
        P("node", "local", None),
        P("node", "local", None),
        P("node", None, "local"),
        P("node", "local"),
    )
    return jax.shard_map(
        per_device,
        mesh=mesh,
        in_specs=placed,
        out_specs=(P("node", "local"), P("node", "local"), P("node", None)),
        check_vma=False,
    )
```

```python
import jax
import jax.numpy as jnp
from jax import lax
from jax.experimental import pallas as pl
from jax.experimental.pallas import tpu as pltpu
from jax.sharding import PartitionSpec as P

TOP = 8
CAP = 10
FLIGHT = 32
STRIDE = 8
TOK = 256
WIDTH = 1792
FF = 1024
MAIN = 8
TAIL = 512
PACKED = WIDTH + TAIL
PAYLOAD = 2 * PACKED
HALF_WIDTH = WIDTH // 2
SENT = 2 * WIDTH + HALF_WIDTH
SPARE = WIDTH + 256
BLOCK = 3 * 512
ROWS = FLIGHT * MAIN
HALF_MAIN = ROWS // 2
HALF = FLIGHT * CAP // 2
TILE = 256
SPAN = 512
STEPS = WIDTH // TILE
ROUTE_SCALE = 2.5
F32 = jnp.float32
BF16 = jnp.bfloat16
NN = (((1,), (0,)), ((), ()))
NT = (((1,), (1,)), ((), ()))
TN = (((0,), (0,)), ((), ()))


def dot(a, b, dims=NN, exact=False):
    precision = lax.Precision.HIGHEST if exact else None
    return lax.dot_general(a, b, dims, precision=precision, preferred_element_type=F32)


def iota(shape, dim):
    return lax.broadcasted_iota(jnp.int32, shape, dim)


def expert_marks(ids_ref, keep_ref, values_ref=None):
    expert = iota((FLIGHT, TOK), 0) * STRIDE
    marks = jnp.zeros((FLIGHT, TOK), F32)
    values = jnp.zeros((FLIGHT, TOK), F32)
    for k in range(TOP):
        hit = (ids_ref[k : k + 1, :] == expert) & (keep_ref[k : k + 1, :] == 1)
        marks = jnp.where(hit, 1.0, marks)
        if values_ref is not None:
            values = jnp.where(hit, values_ref[k : k + 1, :], values)
    return marks, values


def spread_matrix():
    return as_bf16(iota((ROWS, FLIGHT), 0) // MAIN == iota((ROWS, FLIGHT), 1))


def slots_of(marks):
    earlier = as_bf16(iota((TOK, TOK), 0) < iota((TOK, TOK), 1))
    position = dot(marks.astype(BF16), earlier)
    return jnp.where((marks > 0.5) & (position < CAP), position, 31.0)


def picks(slot):
    spread = dot(spread_matrix(), slot.astype(BF16))
    sub = (iota((ROWS, TOK), 0) % MAIN).astype(F32)
    tail_sub = (iota((ROWS, TOK), 0) % 2 + MAIN).astype(F32)
    return spread == sub, spread == tail_sub


def as_bf16(mask):
    return jnp.where(mask, 1.0, 0.0).astype(BF16)


def halves_of(values):
    high = values.astype(BF16)
    return high, (values - high.astype(F32)).astype(BF16)


def weights_of(affinity_ref):
    affinity = affinity_ref[...]
    return ROUTE_SCALE * affinity / jnp.sum(affinity, axis=0, keepdims=True)


def send_kernel(*refs):
    route_refs, (token_ref, cot_ref, out_ref) = refs[:3], refs[3:6]
    ids_ref, keep_ref, affinity_ref, weight_ref, in_ref, packed_ref, route_sem, in_sem, out_sem = refs[6:]
    held = (ids_ref, keep_ref, affinity_ref)
    route = [pltpu.make_async_copy(route_refs[i], held[i], route_sem.at[i]) for i in range(3)]
    for copy in route:
        copy.start()

    def load(i):
        source = (token_ref, cot_ref)[i // 2]
        cols = slice(i % 2 * HALF_WIDTH, (i % 2 + 1) * HALF_WIDTH)
        return pltpu.make_async_copy(source.at[:, cols], in_ref.at[i], in_sem.at[i])

    def store(i):
        cols = slice(i * HALF_WIDTH, (i + 1) * HALF_WIDTH)
        return pltpu.make_async_copy(packed_ref.at[:, cols], out_ref.at[:, cols], out_sem.at[i])

    for i in range(4):
        load(i).start()
    for copy in route:
        copy.wait()
    weight_ref[...] = weights_of(affinity_ref)
    marks, weights = expert_marks(ids_ref, keep_ref, weight_ref)
    slot = slots_of(marks)
    main, unused = picks(slot)
    dense_row = iota((2 * FLIGHT, TOK), 0)
    pair = as_bf16(iota((2 * FLIGHT, FLIGHT), 0) // 2 == iota((2 * FLIGHT, FLIGHT), 1))
    dense = dot(pair, slot.astype(BF16)) == (dense_row % 2 + MAIN).astype(F32)
    place = jnp.concatenate([as_bf16(main), as_bf16(dense)], axis=0)
    high, low = halves_of(weights)
    main_scale, tail_scale = [
        jnp.sum(jnp.where(mask, dot(copies, high) + dot(copies, low), 0.0), axis=1, keepdims=True)
        for mask, copies in ((main, spread_matrix()), (dense, pair))
    ]
    for i in range(4):
        load(i).wait()
    pieces = []
    for i in range(4):
        both = dot(place, in_ref[i])
        first, second = both[:ROWS], both[ROWS:]
        if i >= 2:
            first, second = first * main_scale, second * tail_scale
        packed_ref[:, i * HALF_WIDTH : (i + 1) * HALF_WIDTH] = first.astype(BF16)
        store(i).start()
        pieces.append(second.astype(BF16))
    row, col = iota((ROWS, ROWS), 0), iota((ROWS, ROWS), 1)
    source, expert, which = col // (2 * FLIGHT), col % (2 * FLIGHT) // 2, col % 2
    goal = 4 * (source % 2) + 2 * (source // 2) + which
    spot = as_bf16((row // MAIN == expert) & (row % MAIN == goal))
    packed_ref[:, 2 * WIDTH :] = dot(spot, jnp.concatenate(pieces, axis=0)).astype(BF16)
    store(4).start()
    for i in range(5):
        store(i).wait()


ROOMY = pltpu.CompilerParams(vmem_limit_bytes=60 * 2**20)
LIMITED = pltpu.CompilerParams(vmem_limit_bytes=32 * 2**20)


def vmem(n):
    return [pl.BlockSpec(memory_space=pltpu.VMEM)] * n


def cost(flops, moved):
    return pl.CostEstimate(flops=int(flops), bytes_accessed=int(moved), transcendentals=0)


def send_rows(ids, keep, affinity, tokens, cotangent):
    return pl.pallas_call(
        send_kernel,
        out_shape=jax.ShapeDtypeStruct((ROWS, SENT), BF16),
        in_specs=[pl.BlockSpec(memory_space=pl.ANY)] * 5,
        out_specs=pl.BlockSpec(memory_space=pl.ANY),
        scratch_shapes=[
            pltpu.VMEM((TOP, TOK), jnp.int32),
            pltpu.VMEM((TOP, TOK), jnp.int32),
            pltpu.VMEM((TOP, TOK), F32),
            pltpu.VMEM((TOP, TOK), F32),
            pltpu.VMEM((4, TOK, HALF_WIDTH), BF16),
            pltpu.VMEM((ROWS, SENT), BF16),
            pltpu.SemaphoreType.DMA((3,)),
            pltpu.SemaphoreType.DMA((4,)),
            pltpu.SemaphoreType.DMA((5,)),
        ],
        compiler_params=ROOMY,
        cost_estimate=cost(8 * ROWS * TOK * WIDTH, 2 * TOK * WIDTH * 6),
        name="send_rows",
    )(ids, keep, affinity, tokens, cotangent)


def unpack_half(packed_ref, array, half, out_ref, base):
    rows = pl.ds(pl.multiple_of(half * HALF_MAIN, HALF_MAIN), HALF_MAIN)
    out_ref[base : base + HALF_MAIN, :] = packed_ref[rows, array * WIDTH : (array + 1) * WIDTH]
    tail = packed_ref[rows, 2 * WIDTH :]
    shape = (HALF - HALF_MAIN, HALF_MAIN)
    row, col = iota(shape, 0), iota(shape, 1)
    for h in range(2):
        same = (row // 2 == col // MAIN) & (col % MAIN == 4 * h + 2 * array + row % 2)
        cols = slice(h * HALF_WIDTH, (h + 1) * HALF_WIDTH)
        out_ref[base + HALF_MAIN : base + HALF, cols] = dot(as_bf16(same), tail).astype(BF16)


def partial_kernel(first, at, core_ref, packed_ref, gate_ref, up_ref, keep_ref, *rest):
    if at is not None:
        *send_refs, rows_ref = rest
        core = core_ref[0]
        unpack_half(packed_ref, at, 1 - core, rows_ref, 0)
        unpack_half(packed_ref, at, core, rows_ref, HALF)
    else:
        send_refs, rows_ref = rest, packed_ref
    span = slice(first, first + SPAN)
    sent = []
    for i, weight_ref in enumerate((gate_ref, up_ref)):
        product = dot(rows_ref[...], weight_ref[:, span])
        sent.append(product[:HALF].astype(BF16))
        keep_ref[:, i * SPAN : (i + 1) * SPAN] = product[HALF:]
    sent = jnp.concatenate(sent, axis=1)
    begin = 0
    for send_ref in send_refs:
        send_ref[...] = sent[:, begin : begin + send_ref.shape[1]]
        begin += send_ref.shape[1]


def partial_sums(name, core, packed, at, gate, up, first, pieces):
    shapes = (jax.ShapeDtypeStruct((HALF, 2 * SPAN), F32),)
    shapes += tuple(jax.ShapeDtypeStruct((HALF, width), BF16) for width in pieces)
    if at is not None:
        shapes += (jax.ShapeDtypeStruct((2 * HALF, WIDTH), BF16),)
    return pl.pallas_call(
        lambda *refs: partial_kernel(first, at, *refs),
        out_shape=shapes,
        in_specs=[pl.BlockSpec(memory_space=pltpu.SMEM)] + vmem(3),
        out_specs=tuple(vmem(len(shapes))),
        compiler_params=LIMITED,
        cost_estimate=cost(1e6, 1e4),
        name=name,
    )(core, packed, gate, up)


def grad_kernel(first, core_ref, packed_ref, weight_ref, send_ref, keep_ref, *rest):
    if rest:
        rows_ref = rest[0]
        core = core_ref[0]
        unpack_half(packed_ref, 1, 1 - core, rows_ref, 0)
        unpack_half(packed_ref, 1, core, rows_ref, HALF)
    else:
        rows_ref = packed_ref
    product = dot(rows_ref[...], weight_ref[first : first + SPAN, :], NT)
    send_ref[...] = product[:HALF].astype(BF16)
    keep_ref[...] = product[HALF:]


def grad_sums(name, core, packed, weight, first):
    shapes = (
        jax.ShapeDtypeStruct((HALF, SPAN), BF16),
        jax.ShapeDtypeStruct((HALF, SPAN), F32),
    )
    if first == 0:
        shapes += (jax.ShapeDtypeStruct((2 * HALF, WIDTH), BF16),)
    return pl.pallas_call(
        lambda *refs: grad_kernel(first, *refs),
        out_shape=shapes,
        in_specs=[pl.BlockSpec(memory_space=pltpu.SMEM)] + vmem(2),
        out_specs=tuple(vmem(len(shapes))),
        compiler_params=LIMITED,
        cost_estimate=cost(1e6, 1e4),
        name=name,
    )(core, packed, weight)


def block_products(rows_ref, first, gate_ref, up_ref, down_ref, cols):
    span = slice(first, first + SPAN)
    out = dot(rows_ref[:, :SPAN], down_ref[span, cols])
    back = dot(rows_ref[:, SPAN : 2 * SPAN], gate_ref[cols, span], NT)
    back += dot(rows_ref[:, 2 * SPAN : BLOCK], up_ref[cols, span], NT)
    return out, back


def spread_first_kernel(*refs):
    own_refs, peer_refs = refs[:3], refs[3:6]
    gate_ref, up_ref, down_ref, out_ref, back_ref, rows_ref = refs[6:]
    for i in range(3):
        rows_ref[:HALF, i * SPAN : (i + 1) * SPAN] = own_refs[i][...]
        rows_ref[HALF:, i * SPAN : (i + 1) * SPAN] = peer_refs[i][...]
    for g in range(2):
        cols = slice(g * HALF_WIDTH, (g + 1) * HALF_WIDTH)
        out_ref[:, cols], back_ref[:, cols] = block_products(
            rows_ref, 0, gate_ref, up_ref, down_ref, cols
        )


def spread_first(own, peer, gate, up, down):
    return pl.pallas_call(
        spread_first_kernel,
        out_shape=(
            jax.ShapeDtypeStruct((2 * HALF, WIDTH), F32),
            jax.ShapeDtypeStruct((2 * HALF, WIDTH), F32),
        ),
        in_specs=vmem(9),
        out_specs=tuple(vmem(2)),
        scratch_shapes=[pltpu.VMEM((2 * HALF, BLOCK), BF16)],
        compiler_params=LIMITED,
        cost_estimate=cost(1e6, 1e4),
        name="spread_a",
    )(*own, *peer, gate, up, down)


def pack(core, product_of, sum_ref, packed_ref, at):
    halves = [
        (base, pl.ds(pl.multiple_of(half * HALF_MAIN, HALF_MAIN), HALF_MAIN))
        for base, half in ((0, core), (HALF, 1 - core))
    ]
    tails = {}
    for g in range(4):
        width = min(TAIL, WIDTH - g * TAIL)
        cols = slice(g * TAIL, g * TAIL + width)
        product = (product_of(cols) + sum_ref[:, cols]).astype(BF16)
        for base, rows in halves:
            packed_ref[rows, at + cols.start : at + cols.stop] = product[base : base + HALF_MAIN]
            tail = product[base + HALF_MAIN : base + HALF]
            if width < TAIL:
                rest = jnp.zeros((HALF - HALF_MAIN, TAIL - width), BF16)
                tail = jnp.concatenate([tail, rest], axis=1)
            tails[base, g] = tail
    row, col = iota((HALF_MAIN, HALF_MAIN), 0), iota((HALF_MAIN, HALF_MAIN), 1)
    piece, pair = col // (HALF - HALF_MAIN), col % (HALF - HALF_MAIN)
    place = as_bf16((row // MAIN == pair // 2) & (row % MAIN == 2 * piece + pair % 2))
    for base, rows in halves:
        stacked = jnp.concatenate([tails[base, g] for g in range(4)], axis=0)
        packed_ref[rows, at + WIDTH : at + PACKED] = dot(place, stacked).astype(BF16)


def spread_out_kernel(core_ref, *refs):
    own_refs, peer_refs, (down_ref, sum_ref, packed_ref, rows_ref) = refs[:2], refs[2:4], refs[4:]
    for i in range(2):
        rows_ref[:HALF, i * TILE : (i + 1) * TILE] = own_refs[i][...]
        rows_ref[HALF:, i * TILE : (i + 1) * TILE] = peer_refs[i][...]

    def product_of(cols):
        return dot(rows_ref[...], down_ref[SPAN:, cols])

    pack(core_ref[0], product_of, sum_ref, packed_ref, 0)


def spread_out(core, own, peer, down, out_sum):
    return pl.pallas_call(
        spread_out_kernel,
        out_shape=jax.ShapeDtypeStruct((ROWS, PACKED), BF16),
        in_specs=[pl.BlockSpec(memory_space=pltpu.SMEM)] + vmem(6),
        out_specs=pl.BlockSpec(memory_space=pltpu.VMEM),
        scratch_shapes=[pltpu.VMEM((2 * HALF, SPAN), BF16)],
        compiler_params=LIMITED,
        cost_estimate=cost(1e6, 1e4),
        name="spread_out",
    )(core, *own, *peer, down, out_sum)


def spread_last_kernel(core_ref, own_ref, peer_ref, gate_ref, up_ref, sum_ref, out_rows_ref, packed_ref, rows_ref):
    core = core_ref[0]
    rows_ref[:HALF] = own_ref[:, : 2 * SPAN]
    rows_ref[HALF:] = peer_ref[:, : 2 * SPAN]

    def product_of(cols):
        product = dot(rows_ref[:, :SPAN], gate_ref[cols, SPAN:], NT)
        packed_ref[:, cols] = out_rows_ref[:, cols]
        return product + dot(rows_ref[:, SPAN:], up_ref[cols, SPAN:], NT)

    packed_ref[:, WIDTH:PACKED] = out_rows_ref[:, WIDTH:]

    pack(core, product_of, sum_ref, packed_ref, PACKED)
    for half_ref, half in ((own_ref, core), (peer_ref, 1 - core)):
        carried = half_ref[:, 2 * SPAN :]
        total = jnp.zeros((HALF_MAIN, 128), F32)
        for first, count, each, base in ((0, HALF_MAIN, MAIN, 0), (HALF_MAIN, HALF - HALF_MAIN, 2, MAIN)):
            row, col = iota((HALF_MAIN, count), 0), iota((HALF_MAIN, count), 1)
            lane = iota((count, 128), 1) == base + iota((count, 128), 0) % each
            for part in range(2):
                place = as_bf16((row // MAIN == col // each) & (row % MAIN == 6 + part))
                column = carried[first : first + count, part : part + 1].astype(F32)
                total += dot(place, jnp.where(lane, column, 0.0).astype(BF16))
        rows = pl.ds(pl.multiple_of(half * HALF_MAIN, HALF_MAIN), HALF_MAIN)
        spare = slice(PACKED + SPARE, PACKED + SPARE + 128)
        packed_ref[rows, spare] = (packed_ref[rows, spare].astype(F32) + total).astype(BF16)


def spread_last(core, own, peer, gate, up, back_sum, out_rows):
    return pl.pallas_call(
        spread_last_kernel,
        out_shape=jax.ShapeDtypeStruct((ROWS, PAYLOAD), BF16),
        in_specs=[pl.BlockSpec(memory_space=pltpu.SMEM)] + vmem(6),
        out_specs=pl.BlockSpec(memory_space=pltpu.VMEM),
        scratch_shapes=[pltpu.VMEM((2 * HALF, 2 * SPAN), BF16)],
        compiler_params=LIMITED,
        cost_estimate=cost(1e6, 1e4),
        name="spread_b",
    )(core, own, peer, gate, up, back_sum, out_rows)


def add_kernel(keep_ref, *refs):
    recv_refs, (total_ref, send_ref) = refs[:-2], refs[-2:]
    at = 0
    for recv_ref in recv_refs:
        cols = slice(at, at + recv_ref.shape[1])
        total = keep_ref[:, cols] + recv_ref[...].astype(F32)
        total_ref[:, cols] = total
        send_ref[:, cols] = total.astype(BF16)
        at += recv_ref.shape[1]


def add_halves(name, keep, *recv):
    return pl.pallas_call(
        add_kernel,
        out_shape=(
            jax.ShapeDtypeStruct(keep.shape, F32),
            jax.ShapeDtypeStruct(keep.shape, BF16),
        ),
        in_specs=vmem(1 + len(recv)),
        out_specs=tuple(vmem(2)),
        compiler_params=LIMITED,
        cost_estimate=cost(1e6, 1e4),
        name=name,
    )(keep, *recv)


def block_kernel(total_ref, recv_ref, grad_total_ref, grad_recv_ref, hidden_ref, gate_ref, up_ref, inner_ref):
    pre = total_ref[...] + recv_ref[...].astype(F32)
    gate, up = pre[:, :SPAN], pre[:, SPAN:]
    grad = grad_total_ref[...] + grad_recv_ref[...].astype(F32)
    sigma = jax.nn.sigmoid(gate)
    hidden = gate * sigma * up
    inner_ref[...] = jnp.broadcast_to(jnp.sum(hidden * grad, axis=1, keepdims=True), (HALF, 128))
    hidden_ref[...] = hidden.astype(BF16)
    gate_ref[...] = (grad * up * sigma * (1.0 + gate * (1.0 - sigma))).astype(BF16)
    up_ref[...] = (grad * gate * sigma).astype(BF16)


def hidden_kernel(total_ref, recv_ref, *hidden_refs):
    pre = total_ref[...] + recv_ref[...].astype(F32)
    gate, up = pre[:, :SPAN], pre[:, SPAN:]
    hidden = (gate * jax.nn.sigmoid(gate) * up).astype(BF16)
    for i, hidden_ref in enumerate(hidden_refs):
        hidden_ref[...] = hidden[:, i * TILE : (i + 1) * TILE]


def pair_kernel(total_ref, recv_ref, grad_total_ref, grad_recv_ref, inner_ref, out_ref):
    pre = total_ref[...] + recv_ref[...].astype(F32)
    gate, up = pre[:, :SPAN], pre[:, SPAN:]
    grad = grad_total_ref[...] + grad_recv_ref[...].astype(F32)
    sigma = jax.nn.sigmoid(gate)
    inner = jnp.sum(gate * sigma * up * grad, axis=1, keepdims=True)
    high, low = halves_of(inner + inner_ref[:, :1])
    lane = iota((HALF, 128), 1)
    both = jnp.where(lane == 0, high.astype(F32), jnp.where(lane == 1, low.astype(F32), 0.0))
    out_ref[:, 2 * SPAN :] = both.astype(BF16)
    out_ref[:, :SPAN] = (grad * up * sigma * (1.0 + gate * (1.0 - sigma))).astype(BF16)
    out_ref[:, SPAN : 2 * SPAN] = (grad * gate * sigma).astype(BF16)


def part_of(name, kernel, widths, *operands):
    shapes = [
        jax.ShapeDtypeStruct((HALF, width), F32 if width == 128 else BF16) for width in widths
    ]
    return pl.pallas_call(
        kernel,
        out_shape=tuple(shapes) if len(shapes) > 1 else shapes[0],
        in_specs=vmem(len(operands)),
        out_specs=tuple(vmem(len(shapes))) if len(shapes) > 1 else vmem(1)[0],
        compiler_params=LIMITED,
        cost_estimate=cost(1e6, 1e4),
        name=name,
    )(*operands)


def plan_kernel(ids_ref, keep_ref, affinity_ref, places_ref, slot_ref, weight_ref):
    weight_ref[...] = weights_of(affinity_ref)
    marks, weights = expert_marks(ids_ref, keep_ref, weight_ref)
    slot = slots_of(marks)
    slot_ref[...] = slot
    wide = dot(spread_matrix(), weights.astype(BF16))
    for i, mask in enumerate(picks(slot)):
        places_ref[i] = jnp.where(mask, wide, 0.0).T.astype(BF16)
        places_ref[2 + i] = jnp.where(mask, 1.0, 0.0).T.astype(BF16)


def plan(ids, keep, affinity):
    return pl.pallas_call(
        plan_kernel,
        out_shape=(
            jax.ShapeDtypeStruct((4, TOK, ROWS), BF16),
            jax.ShapeDtypeStruct((FLIGHT, TOK), F32),
            jax.ShapeDtypeStruct((TOP, TOK), F32),
        ),
        in_specs=vmem(3),
        out_specs=tuple(vmem(3)),
        compiler_params=LIMITED,
        cost_estimate=cost(1e6, 1e4),
        name="plan",
    )(ids, keep, affinity)


def combine_kernel(ids_ref, keep_ref, affinity_ref, places_ref, slot_ref, weight_ref, packed_ref, mixed_ref, grad_ref, share_ref, held_ref, sem):
    def store(array, g):
        cols = slice(g * TAIL, min((g + 1) * TAIL, WIDTH))
        target = (mixed_ref, grad_ref)[array]
        return pltpu.make_async_copy(held_ref.at[array, :, cols], target.at[:, cols], sem.at[array, g])

    piece = iota((TOK, ROWS), 1) % MAIN // 2
    for g in range(4):
        cols = slice(g * TAIL, min((g + 1) * TAIL, WIDTH))
        width = cols.stop - cols.start
        for array in range(2):
            at = array * PACKED
            total = dot(places_ref[2 * array], packed_ref[:, at + cols.start : at + cols.stop])
            tail = places_ref[2 * array + 1]
            chosen = jnp.where(piece == g, tail, jnp.zeros_like(tail))
            total += dot(chosen, packed_ref[:, at + WIDTH : at + WIDTH + width])
            held_ref[array, :, cols] = total.astype(BF16)
            store(array, g).start()

    slot = slot_ref[...]
    row, col = iota((FLIGHT, ROWS), 0), iota((FLIGHT, ROWS), 1)
    both = as_bf16((col // MAIN == row) & (col % MAIN >= 6))
    carried = dot(both, packed_ref[:, PACKED + SPARE : PACKED + SPARE + 128])
    by_expert = jnp.zeros((FLIGHT, TOK), F32)
    for s in range(CAP):
        by_expert += jnp.where(slot == float(s), carried[:, s : s + 1], 0.0)
    expert = iota((FLIGHT, TOK), 0) * STRIDE
    for k in range(TOP):
        hit = (ids_ref[k : k + 1, :] == expert) & (keep_ref[k : k + 1, :] == 1)
        share_ref[k : k + 1, :] = jnp.sum(jnp.where(hit, by_expert, 0.0), axis=0, keepdims=True)
    affinity = affinity_ref[...]
    total = jnp.sum(affinity, axis=0, keepdims=True)
    inner = share_ref[...] / weight_ref[...]
    shares = affinity / total
    share_ref[...] = (
        ROUTE_SCALE / total * (inner - jnp.sum(shares * inner, axis=0, keepdims=True))
    )
    for array in range(2):
        for g in range(4):
            store(array, g).wait()


def combine(ids, keep, affinity, planned, packed):
    return pl.pallas_call(
        combine_kernel,
        out_shape=(
            jax.ShapeDtypeStruct((TOK, WIDTH), BF16),
            jax.ShapeDtypeStruct((TOK, WIDTH), BF16),
            jax.ShapeDtypeStruct((TOP, TOK), F32),
        ),
        in_specs=vmem(7),
        out_specs=(pl.BlockSpec(memory_space=pl.ANY),) * 2 + tuple(vmem(1)),
        scratch_shapes=[
            pltpu.VMEM((2, TOK, WIDTH), BF16),
            pltpu.SemaphoreType.DMA((2, 4)),
        ],
        compiler_params=LIMITED,
        cost_estimate=cost(8 * ROWS * TOK * WIDTH, 2 * TOK * WIDTH * 4),
        name="combine",
    )(ids, keep, affinity, *planned, packed)


def exchange(packed):
    return lax.all_to_all(packed, "node", split_axis=0, concat_axis=0, tiled=True)


def swap(values, distance):
    return lax.ppermute(values, "local", [(i, i ^ distance) for i in range(4)])


def per_device(tokens, expert_ids, keep_flags, affinity, w_gate, w_up, w_down, cotangent):
    core = (lax.axis_index("local") % 2).astype(jnp.int32).reshape(1)
    ids, keep, affinity_t = expert_ids.T, keep_flags.T, affinity.T
    w_gate, w_up, w_down = w_gate[0], w_up[0], w_down[0]

    payload = send_rows(ids, keep, affinity_t, tokens, cotangent)
    payload, core = lax.optimization_barrier((payload, core))
    rows = exchange(payload)

    send_g, own_g, grad_rows = grad_sums("grad_a", core, rows, w_down, 0)
    total_g, send_g = add_halves("add_ga", own_g, swap(send_g, 1))
    rows, send_g = lax.optimization_barrier((rows, send_g))
    recv_g = swap(send_g, 2)
    own_a, *sends, unpacked = partial_sums("pre_a", core, rows, 0, w_gate, w_up, 0, (384, 384, 256))
    total_a, send_a = add_halves("add_a", own_a, *[swap(part, 1) for part in sends])
    recv_a = swap(send_a, 2)
    unpacked, recv_g = lax.optimization_barrier((unpacked, recv_g))
    own_b, *sends = partial_sums("pre_b", core, unpacked, None, w_gate, w_up, SPAN, (SPAN, SPAN))
    total_b, send_b = add_halves("add_b", own_b, *[swap(part, 1) for part in sends])
    recv_b = swap(send_b, 2)
    send_h, own_h = grad_sums("grad_b", core, grad_rows, w_down, SPAN)
    total_h, send_h = add_halves("add_gb", own_h, swap(send_h, 1))
    total_a, send_h = lax.optimization_barrier((total_a, send_h))
    recv_h = swap(send_h, 2)
    route, total_b = lax.optimization_barrier(((ids, keep, affinity_t), total_b))
    planned = plan(*route)

    *block_a, inner = part_of(
        "block_a", block_kernel, (SPAN, SPAN, SPAN, 128), total_a, recv_a, total_g, recv_g
    )
    peer_a = [swap(part, 1) for part in block_a]
    out_sum, back_sum = spread_first(block_a, peer_a, w_gate, w_up, w_down)
    recv_b, out_sum, back_sum, planned = lax.optimization_barrier((recv_b, out_sum, back_sum, planned))
    hidden_b = part_of("hidden_b", hidden_kernel, (TILE, TILE), total_b, recv_b)
    out_rows = spread_out(core, hidden_b, [swap(part, 1) for part in hidden_b], w_down, out_sum)
    recv_h, out_rows = lax.optimization_barrier((recv_h, out_rows))
    pair_b = part_of(
        "pair_b", pair_kernel, (2 * SPAN + 128,), total_b, recv_b, total_h, recv_h, inner
    )
    payload = spread_last(core, pair_b, swap(pair_b, 1), w_gate, w_up, back_sum, out_rows)
    rows = exchange(payload)
    mixed, token_grad, affinity_grad = combine(ids, keep, affinity_t, planned, rows)
    return mixed, token_grad, affinity_grad.T


def solution(mesh):
    placed = (
        P("node", "local"),
        P("node", None),
        P("node", None),
        P("node", None),
        P("node", "local", None),
        P("node", "local", None),
        P("node", None, "local"),
        P("node", "local"),
    )
    return jax.shard_map(
        per_device,
        mesh=mesh,
        in_specs=placed,
        out_specs=(P("node", "local"), P("node", "local"), P("node", None)),
        check_vma=False,
    )
```
